32 devices in a mesh: grp: 2 (over y), ep: 8 (over z, x), seq: 1, rep: 2 (over core).
Axes of the slice: x: 2, y: 2, z: 4, core: 2. Of those that a mesh axis runs over, the one named last changes fastest.
Arguments:
- hidden_in: bfloat16 [1024, 2048], P(('grp', 'ep', 'rep'), 'seq'), parts along dimension 0, may hold values from -64 to 64
- row_counts: int32 [32], P(('grp', 'ep', 'rep')), parts along dimension 0, may hold values from 24 to 32, as said below
- qkv_new: bfloat16 [1024, 3, 2048], P(('grp', 'ep', 'rep')), parts along dimension 0, may hold values from -6 to 6
- cache_len: int32 [16, 64], P('grp', ('rep', 'seq')), parts along dimension 0, may hold values from 1 to 128, as said below
- kv_cache: bfloat16 [2, 16, 64, 128, 2048], P(None, 'grp', ('rep', 'seq'), None, 'ep'), parts along dimension 1, may hold values from -128 to 128
- w_out: bfloat16 [2048, 2048], P('ep', 'seq'), may hold values from -0.125 to 0.125
- moe_gain: float32 [2048], replicated, may hold values from 0.1 to 1.9
- w_in: bfloat16 [16, 2048, 2, 1408], P(('ep', 'rep'), None, None, 'seq'), may hold values from -0.125 to 0.125
- w_down: bfloat16 [16, 1408, 2048], P(('ep', 'rep'), 'seq'), may hold values from -0.15625 to 0.15625
- route_ids: int32 [1024, 6], P(('grp', 'ep', 'rep')), parts along dimension 0, may hold values from 0 to 15, all different within a row; in each aligned block of 32 rows (0 to 31, 32 to 63, ...) at most 24 rows name the same one
- route_weight: bfloat16 [1024, 6], P(('grp', 'ep', 'rep')), parts along dimension 0, may hold values from 0.049804688 to 0.44921875
Outputs:
- mixed: bfloat16 [1024, 2048], P(('grp', 'ep', 'rep'), 'seq'), parts along dimension 0
The draws below stay inside these ranges and needn't reach their ends.
There are 2 independent parts, one for each index of `grp`. The reference program is written for one: setup_inputs(seed, part) draws one part's arguments, and reference() takes and returns one part's arrays. A program takes and returns all parts, laid end to end along the dimension named above; an argument that names none is the same for every part. Nothing has to cross between parts.
Inputs may be any that keep to these rules, and one draw needn't show every extreme that they name: The first row_counts[b] slots of block b are live; some block is full. `cache_len`: some row has 128 cached positions. `route_ids`: a row's 6 experts differ; among the 32 rows of one block no expert is named by more than 24 rows, and in some block one is named by exactly 24.
All inputs are finite; a program needn't handle non-finite values.
Results may differ from the reference program's by a relative error of at most 0.0053.
Values may be sent and summed in bfloat16 or wider, within the bound.
No kernel may reach another device: no remote copies, remote signals or barrier semaphores. Data moves between devices by JAX's collectives and lax.ppermute only.
A program may use at most 192 MiB of HBM per device.

```python
import math
import jax
import jax.numpy as jnp
import numpy as np
from jax import lax

D = 2048
FF = 1408
HEADS = 16
HEAD_DIM = 128
TOPK = 6
RB = 32
L = 128
ROWS = 512
EXPERTS = 16
CAP = 24
N_EP = 8
N_REP = 2


def make_lengths(key):
    part_keys = jax.random.split(jax.random.fold_in(key, 5), 2)
    lengths = jax.random.randint(part_keys[0], (ROWS,), 1, L + 1)
    longest_row = jax.random.randint(part_keys[1], (), 0, ROWS)
    return jnp.where(jnp.arange(ROWS) == longest_row, L, lengths).astype(jnp.int32)


def make_fresh(key):
    fresh_key = jax.random.fold_in(key, 7)
    drawn = jax.random.truncated_normal(fresh_key, -6.0, 6.0, (ROWS, 3, HEADS * HEAD_DIM), jnp.float32)
    return drawn


def draw_hidden_in(key, part):
    part_keys = jax.random.split(jax.random.fold_in(key, 11), 2)
    base_draw = jax.random.truncated_normal(part_keys[0], -6.0, 6.0, (ROWS, D), jnp.float32)
    column_scale = jnp.exp(jax.random.uniform(part_keys[1], (D,), jnp.float32, 0.0, math.log(10.0))) / 4.0
    column_ramp = 1.0 + 2.0 * jnp.arange(D, dtype=jnp.float32) / D
    drawn = base_draw * column_scale * jnp.sqrt(column_ramp)
    return jnp.clip(drawn, -60.0, 60.0).astype(jnp.bfloat16)


def draw_row_counts(key, part):
    part_keys = jax.random.split(jax.random.fold_in(key, 3), 2)
    blocks = N_EP * N_REP
    counts = jax.random.randint(part_keys[0], (blocks,), RB - RB // 4, RB + 1)
    full_block = jax.random.randint(part_keys[1], (), 0, blocks)
    return jnp.where(jnp.arange(blocks) == full_block, RB, counts).astype(jnp.int32)


def draw_qkv_new(key, part):
    return make_fresh(key).astype(jnp.bfloat16)


def draw_cache_len(key, part):
    return make_lengths(key).reshape(N_EP, N_REP * RB)


def draw_kv_cache(key, part):
    head_width = HEADS * HEAD_DIM
    part_keys = jax.random.split(jax.random.fold_in(key, 9), 2)
    cache_keys = jax.random.truncated_normal(part_keys[0], -6.0, 6.0, (ROWS, L, head_width), jnp.float32)
    cache_values = 2.0 * jax.random.truncated_normal(part_keys[1], -6.0, 6.0, (ROWS, L, head_width), jnp.float32)
    stacked = jnp.stack([cache_keys, cache_values]).reshape(2, N_EP, N_REP * RB, L, head_width)
    return jnp.clip(stacked, -128.0, 128.0).astype(jnp.bfloat16)


def level_of(key, shape, shards, least, high):
    factor_of, own = 1.0, jax.random.fold_in(key, 6)
    for dim, blocks in shards:
        steps = jnp.exp(jax.random.uniform(jax.random.fold_in(own, dim), (blocks,), jnp.float32, least / len(shards), high / len(shards)))
        factor_of = factor_of * jnp.repeat(steps, shape[dim] // blocks).reshape([-1 if axis == dim else 1 for axis in range(len(shape))])
    return factor_of


def shared_out(key, own, number, rows, number_of, top, limit, slope):
    ranking = jax.random.permutation(key, number_of)
    packed, usual = portions_of(number_of, rows * top, limit, slope, True), portions_of(number_of, rows * top, limit, slope, False)
    places = jnp.arange(number_of)

    def named(tallies, turn):
        used = int((tallies > 0).sum())
        fixed = max(1, used // 4)
        moved = fixed + (places - fixed + turn * (used - fixed)) % max(1, number_of - fixed)
        return jnp.zeros((number_of,), jnp.int32).at[ranking[jnp.where(places < fixed, places, moved)]].set(jnp.asarray(tallies, jnp.int32))

    tallies = jnp.where(number % 4 == 0, named(packed, number // 4), named(usual, number - number // 4 - 1))
    mixed = jax.random.permutation(jax.random.fold_in(own, 3), number_of)
    source_of, taker = mixed[0:number_of // 2 * 2:2], mixed[1:number_of // 2 * 2:2]
    margin = jnp.minimum(tallies[source_of] - 1, limit - tallies[taker]) // 2
    margin = jnp.where((source_of == ranking[0]) | (taker == ranking[0]) | (tallies[taker] == 0), 0, jnp.maximum(margin, 0))
    moved = jax.random.randint(jax.random.fold_in(own, 4), (number_of // 2,), 0, 1 << 20) % (margin + 1)
    tallies = tallies.at[source_of].add(-moved).at[taker].add(moved)
    items = jnp.searchsorted(jnp.cumsum(tallies), jnp.arange(rows * top), side="right").astype(jnp.int32)
    listing = items.reshape(top, rows).T
    listing = listing[jax.random.permutation(jax.random.fold_in(own, 1), rows)]
    turn = jax.random.randint(jax.random.fold_in(own, 2), (rows, 1), 0, top)
    return jnp.take_along_axis(listing, (jnp.arange(top)[None, :] + turn) % top, axis=1)


def portions_of(count, total, limit, slope, full):
    weights = [(1 << 20) // math.isqrt(rank ** slope) + 1 for rank in range(1, count + 1)]
    largest = limit if full else min(limit, max(-(-total // count), total * weights[0] // sum(weights)))
    least = 1 if total - largest >= count - 1 else 0
    given, rest = [largest] + [least] * (count - 1), total - largest - least * (count - 1)
    while rest > 0:
        free = [i for i in range(1, count) if given[i] < largest] or [i for i in range(1, count) if given[i] < limit]
        mass, remaining = sum([weights[i] for i in free]), rest
        for i in free:
            more = min(limit - given[i], max(1, remaining * weights[i] // mass), rest)
            given[i] = given[i] + more
            rest = rest - more
    return np.array(given)


def scatter_about(rng, dims, deviation, limit, cuts=(), kind=jnp.bfloat16):
    values = deviation * jax.random.normal(rng, dims, jnp.float32)
    if cuts:
        values = values * level_of(rng, dims, cuts, -0.22, 0.18)
    return jnp.clip(values, -limit, limit).astype(kind)


def setup_inputs(seed: int = 0, part: int = 0) -> dict:
    seeds = jax.random.split(jax.random.key(seed), 12)
    own_keys = jax.random.split(jax.random.fold_in(seeds[11], part), 12)
    hidden_in = draw_hidden_in(jax.random.fold_in(jax.random.fold_in(seeds[11], part), 71), part)
    row_counts = draw_row_counts(jax.random.fold_in(jax.random.fold_in(seeds[11], part), 71), part)
    qkv_new = draw_qkv_new(jax.random.fold_in(jax.random.fold_in(seeds[11], part), 71), part)
    cache_len = draw_cache_len(jax.random.fold_in(jax.random.fold_in(seeds[11], part), 71), part)
    kv_cache = draw_kv_cache(jax.random.fold_in(jax.random.fold_in(seeds[11], part), 71), part)
    w_out = scatter_about(seeds[5], (HEADS * HEAD_DIM, D), (HEADS * HEAD_DIM) ** -0.5, 0.125, ((0, 8),))
    moe_gain = jnp.clip(1.0 + 0.18 * jax.random.normal(seeds[6], (D,), jnp.float32), 0.1, 1.9)
    w_in = scatter_about(seeds[7], (EXPERTS, D, 2, FF), D ** -0.5, 0.125, ((0, 16),))
    w_down = scatter_about(seeds[8], (EXPERTS, FF, D), FF ** -0.5, 0.15625, ((0, 16),))
    route_ids_keys = jax.random.split(jax.random.fold_in(own_keys[9], 1), ROWS // RB)
    route_ids_turns = jax.random.permutation(jax.random.fold_in(own_keys[9], 3), ROWS // RB)
    route_ids = jax.vmap(lambda own, number: shared_out(jax.random.fold_in(own_keys[9], 2), own, number, RB, EXPERTS, TOPK, CAP, 2))(route_ids_keys, route_ids_turns).reshape((ROWS, TOPK))
    route_weight = jnp.clip(0.049804688 + 0.39941406 * jax.random.uniform(own_keys[10], (ROWS, TOPK), jnp.float32) ** level_of(own_keys[10], (ROWS, TOPK), ((0, 16),), -0.2, 0.2), 0.049804688, 0.44921875).astype(jnp.bfloat16)
    return {"hidden_in": hidden_in, "row_counts": row_counts, "qkv_new": qkv_new, "cache_len": cache_len, "kv_cache": kv_cache, "w_out": w_out, "moe_gain": moe_gain, "w_in": w_in, "w_down": w_down, "route_ids": route_ids, "route_weight": route_weight}


epsilon = 1e-06
masked_score = -1e+30

def reference(hidden_in, row_counts, qkv_new, cache_len, kv_cache, w_out, moe_gain, w_in, w_down, route_ids, route_weight):
    head_width = HEADS * HEAD_DIM
    blocks = N_EP * N_REP
    row_index = jnp.arange(ROWS, dtype=jnp.int32)
    block_of = row_index // RB
    counts_row = lax.optimization_barrier(jnp.sum(jnp.where(block_of[:, None] == jnp.arange(blocks, dtype=jnp.int32)[None, :], row_counts[None, :], 0), axis=1))
    is_live = row_index % RB < counts_row
    lengths = cache_len.reshape(ROWS)
    score_scale = 1.0 / math.sqrt(HEAD_DIM)
    fresh_rows = qkv_new.astype(jnp.float32).reshape(ROWS, 3, HEADS, HEAD_DIM)
    queries = fresh_rows[:, 0]
    own_score = lax.optimization_barrier(jnp.sum(queries * fresh_rows[:, 1], axis=2)) * score_scale
    cached = kv_cache.reshape(2, ROWS // RB, RB, L, HEADS, HEAD_DIM)
    group_count = ROWS // RB

    def attend_block(inputs):
        query_rows, key_rows, value_rows, length_rows, own_rows, value_fresh = inputs
        scores = jnp.einsum('bhd,blhd->bhl', query_rows, key_rows.astype(jnp.float32), precision=lax.Precision.HIGHEST) * score_scale
        position = jnp.arange(L, dtype=jnp.int32)
        in_cache = position[None, None, :] < length_rows[:, None, None]
        scores = jnp.where(in_cache, scores, masked_score)
        highest = jnp.maximum(lax.optimization_barrier(jnp.max(scores, axis=2)), own_rows)
        weights = jnp.where(in_cache, jnp.exp(scores - highest[..., None]), 0.0)
        rounded = lax.optimization_barrier(weights.astype(jnp.bfloat16)).astype(jnp.float32)
        own_weight = jnp.exp(own_rows - highest)
        denominator = lax.optimization_barrier(jnp.sum(weights, axis=2)) + own_weight
        summed = jnp.einsum('bhl,blhd->bhd', rounded, value_rows.astype(jnp.float32), precision=lax.Precision.HIGHEST) + own_weight[..., None] * value_fresh
        return summed / denominator[..., None]
    attended = lax.map(attend_block, (queries.reshape(group_count, RB, HEADS, HEAD_DIM), cached[0], cached[1], lengths.reshape(group_count, RB), own_score.reshape(group_count, RB, HEADS), fresh_rows[:, 2].reshape(group_count, RB, HEADS, HEAD_DIM)))
    attended = attended.reshape(ROWS, head_width).astype(jnp.bfloat16)
    attn_out = jnp.dot(attended, w_out, preferred_element_type=jnp.float32)
    residual = (hidden_in.astype(jnp.float32) + attn_out).astype(jnp.bfloat16)
    residual_wide = lax.optimization_barrier(residual).astype(jnp.float32)
    inverse_rms = lax.rsqrt(lax.optimization_barrier(jnp.mean(residual_wide * residual_wide, axis=1)) + epsilon)
    normed = (residual_wide * inverse_rms[:, None] * moe_gain).astype(jnp.bfloat16)
    expert_ids = jnp.arange(EXPERTS, dtype=jnp.int32)
    named_hits = (route_ids[:, :, None] == expert_ids[None, None, :]) & is_live[:, None, None]
    coeffs = lax.optimization_barrier(jnp.sum(jnp.where(named_hits, route_weight.astype(jnp.float32)[:, :, None], 0.0), axis=1))
    chosen = jnp.any(named_hits, axis=1)
    slot_limit = EXPERTS * CAP

    def one_expert(running, expert):
        order_key = jnp.where(chosen[:, expert], row_index, row_index + ROWS)
        picked = jnp.argsort(order_key)[:slot_limit].astype(jnp.int32)
        rows_in = normed[picked]
        weight_in = lax.dynamic_index_in_dim(w_in, expert, 0, keepdims=False).reshape(D, 2 * FF)
        gate_up = jnp.dot(rows_in, weight_in, preferred_element_type=jnp.float32).reshape(slot_limit, 2, FF)
        hidden_units = (jax.nn.silu(gate_up[:, 0]) * gate_up[:, 1]).astype(jnp.bfloat16)
        weight_down = lax.dynamic_index_in_dim(w_down, expert, 0, keepdims=False)
        produced = jnp.dot(hidden_units, weight_down, preferred_element_type=jnp.float32).astype(jnp.bfloat16)
        produced = lax.optimization_barrier(produced).astype(jnp.float32)
        factor = coeffs[picked, expert]
        return (running.at[picked].add(factor[:, None] * produced), None)
    moe_out, _ = lax.scan(one_expert, jnp.zeros((ROWS, D), jnp.float32), expert_ids)
    mixed = jnp.where(is_live[:, None], residual_wide + moe_out, 0.0).astype(jnp.bfloat16)
    return mixed
```

```python
import functools
import math

import jax
import jax.numpy as jnp
from jax import lax
from jax.experimental import pallas as pl
from jax.experimental.pallas import tpu as pltpu
from jax.sharding import PartitionSpec as P

HEAD_DIM = 128
LANES = 128
PART = 8
ROWS = 32
epsilon = 1e-06
masked_score = -1e30


def attend_kernel(q_ref, len_ref, k_ref, v_ref, o_ref, m_ref, l_ref):
    rows, positions, width = k_ref.shape[1:]
    heads = width // HEAD_DIM
    part = math.gcd(rows, PART)
    parts = rows // part
    group = heads * part
    q = q_ref[...].astype(jnp.float32)
    head_of = lax.broadcasted_iota(jnp.int32, (part, width), 1) // HEAD_DIM
    which = lax.broadcasted_iota(jnp.int32, (group, positions), 0) % part
    pieces = []
    for g in range(parts):
        mine = q[g * part : (g + 1) * part]
        spread = jnp.concatenate(
            [jnp.where(head_of == h, mine, 0.0) for h in range(heads)], axis=0
        ).astype(jnp.bfloat16)
        keys = k_ref[0, g * part : (g + 1) * part].reshape(part * positions, width)
        every = lax.dot_general(
            spread, keys, (((1,), (1,)), ((), ())), preferred_element_type=jnp.float32
        )
        scores = every[:, :positions]
        for row in range(1, part):
            scores = jnp.where(
                which == row, every[:, row * positions : (row + 1) * positions], scores
            )
        pieces.append(scores)
    scores = jnp.concatenate(pieces, axis=0) * (1.0 / math.sqrt(HEAD_DIM))
    lengths = len_ref[...]
    lengths = jnp.concatenate(
        [lengths[g * part : (g + 1) * part] for g in range(parts) for h in range(heads)], axis=0
    )
    in_cache = lax.broadcasted_iota(jnp.int32, scores.shape, 1) < lengths
    scores = jnp.where(in_cache, scores, masked_score)
    highest = jnp.max(scores, axis=1, keepdims=True)
    weights = jnp.where(in_cache, jnp.exp(scores - highest), 0.0)
    total = jnp.sum(weights, axis=1, keepdims=True)
    for g in range(parts):
        mine = weights[g * group : (g + 1) * group]
        blocks = jnp.concatenate(
            [jnp.where(which == row, mine, 0.0).astype(jnp.bfloat16) for row in range(part)],
            axis=1,
        )
        values = v_ref[0, g * part : (g + 1) * part].reshape(part * positions, width)
        summed = lax.dot_general(
            blocks, values, (((1,), (0,)), ((), ())), preferred_element_type=jnp.float32
        )
        for h in range(heads):
            at = g * group + h * part
            place = (pl.ds(g * part, part), pl.ds(h * HEAD_DIM, HEAD_DIM))
            o_ref[place] = summed[
                h * part : (h + 1) * part, h * HEAD_DIM : (h + 1) * HEAD_DIM
            ]
            m_ref[place] = jnp.broadcast_to(highest[at : at + part], (part, HEAD_DIM))
            l_ref[place] = jnp.broadcast_to(total[at : at + part], (part, HEAD_DIM))


def attend(q, lengths, kv):
    _, n, positions, width = kv.shape
    rows = math.gcd(n, ROWS)
    wide = jax.ShapeDtypeStruct((n, width), jnp.float32)
    return pl.pallas_call(
        attend_kernel,
        grid=(n // rows,),
        in_specs=[
            pl.BlockSpec((rows, width), lambda i: (i, 0)),
            pl.BlockSpec((rows, 1), lambda i: (i, 0)),
            pl.BlockSpec((1, rows, positions, width), lambda i: (0, i, 0, 0)),
            pl.BlockSpec((1, rows, positions, width), lambda i: (1, i, 0, 0)),
        ],
        out_specs=[pl.BlockSpec((rows, width), lambda i: (i, 0))] * 3,
        out_shape=[wide] * 3,
        compiler_params=pltpu.CompilerParams(vmem_limit_bytes=28 << 20),
        cost_estimate=pl.CostEstimate(
            flops=4 * n * positions * width,
            bytes_accessed=4 * n * positions * width,
            transcendentals=0,
        ),
    )(q, lengths, kv, kv)


def expert_kernel(first, x_ref, c_ref, w_ref, d_ref, y_ref, h_ref):
    step = pl.program_id(0)
    tile = w_ref.shape[2]

    @pl.when(step < first)
    def _():
        both = jnp.concatenate([w_ref[0], w_ref[1]], axis=1)
        gate_up = jnp.dot(x_ref[...], both, preferred_element_type=jnp.float32)
        gate, up = gate_up[:, :tile], gate_up[:, tile:]
        h_ref[step] = (gate / (1.0 + jnp.exp(-gate)) * up).astype(jnp.bfloat16)

    @pl.when(step >= first)
    def _():
        units = jnp.concatenate([h_ref[i] for i in range(first)], axis=1)
        y = jnp.dot(units, d_ref[...], preferred_element_type=jnp.float32)
        y = y.astype(jnp.bfloat16).astype(jnp.float32) * c_ref[...]
        y_ref[...] = y.astype(jnp.bfloat16)


def expert(x, coeffs, w_both, w_down):
    rows = x.shape[0]
    _, depth, units = w_both.shape
    width = w_down.shape[1]
    tile = LANES if units % LANES == 0 else units
    out_tile = math.gcd(width, 256)
    first, second = units // tile, width // out_tile
    return pl.pallas_call(
        functools.partial(expert_kernel, first),
        grid=(first + second,),
        in_specs=[
            pl.BlockSpec((rows, depth), lambda i: (0, 0)),
            pl.BlockSpec((rows, 1), lambda i: (0, 0)),
            pl.BlockSpec((2, depth, tile), lambda i: (0, 0, jnp.minimum(i, first - 1))),
            pl.BlockSpec((units, out_tile), lambda i: (0, jnp.maximum(i - first, 0))),
        ],
        out_specs=pl.BlockSpec((rows, out_tile), lambda i: (0, jnp.maximum(i - first, 0))),
        out_shape=jax.ShapeDtypeStruct((rows, width), jnp.bfloat16),
        scratch_shapes=[pltpu.VMEM((first, rows, tile), jnp.bfloat16)],
        compiler_params=pltpu.CompilerParams(vmem_limit_bytes=28 << 20),
        cost_estimate=pl.CostEstimate(
            flops=6 * rows * depth * units,
            bytes_accessed=2 * (3 * depth * units + 2 * rows * depth),
            transcendentals=rows * units,
        ),
    )(x, coeffs, w_both, w_down)


def split_three(v):
    parts = []
    for _ in range(3):
        part = lax.reduce_precision(v, 8, 7)
        parts.append(part.astype(jnp.bfloat16))
        v = v - part
    return jnp.stack(parts, axis=-1)


def local(
    hidden_in,
    row_counts,
    qkv_new,
    cache_len,
    kv_cache,
    w_out,
    moe_gain,
    w_in,
    w_down,
    route_ids,
    route_weight,
):
    wide = jnp.float32
    narrow = jnp.bfloat16
    tok_rows, feat_local = hidden_in.shape
    owners = lax.axis_size("ep")
    reps = lax.axis_size("rep")
    parts_seq = lax.axis_size("seq")
    width_local = kv_cache.shape[-1]
    heads_local = width_local // HEAD_DIM
    positions = kv_cache.shape[3]
    share_rows = tok_rows // parts_seq
    attend_rows = owners * share_rows
    inner = 2 if owners % 2 == 0 else 1
    outer = owners // inner
    me = lax.axis_index("ep")
    outer_me, inner_me = me // inner, me % inner

    def across(v):
        return lax.ppermute(v, "ep", [(i, i ^ 1) for i in range(owners)])

    def along(v, k):
        pairs = [
            (i, (i // inner + k) % outer * inner + i % inner) for i in range(owners)
        ]
        return lax.ppermute(v, "ep", pairs)

    def other(v):
        return lax.ppermute(v, "rep", [(i, (i + 1) % reps) for i in range(reps)])

    def rows_of_seq(v, axis):
        return lax.dynamic_slice_in_dim(v, lax.axis_index("seq") * share_rows, share_rows, axis)

    fresh = qkv_new.reshape(tok_rows, 3, owners, width_local)
    sent_q = fresh[:, 0].transpose(1, 0, 2)
    queries = lax.all_to_all(sent_q, "ep", split_axis=0, concat_axis=0, tiled=True)
    queries = rows_of_seq(queries, 1).reshape(attend_rows, width_local)

    heads = qkv_new.reshape(tok_rows, 3, owners, heads_local, HEAD_DIM).astype(wide)
    own = jnp.sum(heads[:, 0] * heads[:, 1], axis=-1) * (1.0 / math.sqrt(HEAD_DIM))
    own = split_three(own).reshape(tok_rows, owners, heads_local * 3)
    own = jnp.pad(own, ((0, 0), (0, 0), (0, LANES - heads_local * 3)))
    sent_v = jnp.concatenate([fresh[:, 2], own], axis=2).transpose(1, 0, 2)
    sent_v, queries = lax.optimization_barrier((sent_v, queries))
    values = lax.all_to_all(sent_v, "ep", split_axis=0, concat_axis=0, tiled=True)
    values = rows_of_seq(values, 1).reshape(attend_rows, width_local + LANES)

    kv = kv_cache.reshape(2, attend_rows, positions, width_local)
    summed, highest, total = attend(queries, cache_len.reshape(attend_rows, 1), kv)
    shape = (attend_rows, heads_local, HEAD_DIM)
    own = jnp.sum(
        values[:, width_local : width_local + heads_local * 3]
        .reshape(attend_rows, heads_local, 3)
        .astype(wide),
        axis=2,
    )[:, :, None]
    highest = highest.reshape(shape)
    top = jnp.maximum(highest, own)
    scale = jnp.exp(highest - top)
    own_weight = jnp.exp(own - top)
    value_new = values[:, :width_local].reshape(shape).astype(wide)
    attended = (summed.reshape(shape) * scale + own_weight * value_new) / (
        total.reshape(shape) * scale + own_weight
    )
    attended = attended.astype(narrow).reshape(owners, share_rows, width_local)
    attended = lax.all_gather(attended, "seq", axis=1, tiled=True)

    attended = attended.reshape(outer, inner, tok_rows, width_local)
    if inner == 2:
        first = inner_me == 0
        kept = jnp.where(first, attended[:, 0], attended[:, 1])
        given = jnp.where(first, attended[:, 1], attended[:, 0])
        joined = jnp.concatenate([kept, across(given)], axis=2)
        if reps == 2:
            half = w_out.shape[0] // 2
            rep_first = lax.axis_index("rep") == 0
            mine = across(jnp.where(rep_first, w_out[:half], w_out[half:]))
            theirs = other(mine)
            both = jnp.concatenate(
                [jnp.where(rep_first, mine, theirs), jnp.where(rep_first, theirs, mine)], axis=0
            )
        else:
            both = across(w_out)
        w_pair = jnp.concatenate([w_out, both], axis=0)
    else:
        joined, w_pair = attended[:, 0], w_out
    turned = lax.dynamic_slice_in_dim(
        jnp.concatenate([joined, joined], axis=0), outer_me, outer, 0
    )
    partial_out = jnp.dot(
        turned.reshape(outer * tok_rows, -1), w_pair, preferred_element_type=wide
    ).reshape(outer, tok_rows, feat_local)
    attn_out = partial_out[0]
    for k in range(1, outer):
        attn_out = attn_out + along(partial_out[k].astype(narrow), k).astype(wide)
    residual = (hidden_in.astype(wide) + attn_out).astype(narrow)
    residual_wide = residual.astype(wide)

    is_live = jnp.arange(tok_rows, dtype=jnp.int32) < row_counts[0]
    experts_local = w_in.shape[0]
    expert_total = owners * reps * experts_local
    hits = route_ids[:, :, None] == jnp.arange(expert_total, dtype=jnp.int32)[None, None, :]
    hits = hits & is_live[:, None, None]
    coeffs = jnp.sum(jnp.where(hits, route_weight.astype(wide)[:, :, None], 0.0), axis=1)
    lanes = -(-expert_total // LANES) * LANES
    coeffs = jnp.pad(coeffs, ((0, 0), (0, lanes - expert_total))).astype(narrow)
    full_rows = lax.all_gather(residual, "seq", axis=1, tiled=True).astype(wide)
    width = full_rows.shape[1]
    inverse_rms = lax.rsqrt(jnp.mean(full_rows * full_rows, axis=1) + epsilon)
    normed = (full_rows * inverse_rms[:, None] * moe_gain).astype(narrow)
    packed = jnp.concatenate([normed, coeffs], axis=1)
    slots = [packed] + [along(packed, k) for k in range(1, outer)]
    if inner == 2:
        slots = slots + [across(s) for s in slots]
    if reps == 2:
        slots = slots + [other(s) for s in slots]
    arrived = jnp.concatenate(slots, axis=0)
    rows_in = arrived[:, :width]
    gates = arrived[:, width:].astype(wide)
    first_expert = (me * reps + lax.axis_index("rep")) * experts_local
    produced = None
    for j in range(experts_local):
        mine = jnp.arange(lanes, dtype=jnp.int32)[None, :] == first_expert + j
        factor = jnp.sum(jnp.where(mine, gates, 0.0), axis=1, keepdims=True)
        w_both = w_in[j].transpose(1, 0, 2)
        part = expert(rows_in, factor, w_both, w_down[j])
        produced = part if produced is None else produced + part
    if parts_seq > 1:
        produced = lax.psum_scatter(
            produced.astype(wide), "seq", scatter_dimension=1, tiled=True
        ).astype(narrow)

    produced = produced.reshape(reps, inner, outer, tok_rows, feat_local)
    if reps == 2:
        merged = produced[0].astype(wide) + other(produced[1]).astype(wide)
    else:
        merged = produced[0].astype(wide)
    cut = feat_local // 2

    def inner_sum(v):
        if inner == 1:
            return v[0]
        return v[0] + across(v[1].astype(narrow)).astype(wide)

    def outer_sum(v):
        result = v[:, 0]
        for k in range(1, outer):
            result = result + along(v[:, k].astype(narrow), -k).astype(wide)
        return result

    left = outer_sum(inner_sum(merged[..., :cut])[None])[0]
    right = inner_sum(outer_sum(merged[..., cut:]))
    moe_out = jnp.concatenate([left, right], axis=1)
    return jnp.where(is_live[:, None], residual_wide + moe_out, 0.0).astype(narrow)


def solution(mesh):
    placed = (
        P(("grp", "ep", "rep"), "seq"),
        P(("grp", "ep", "rep")),
        P(("grp", "ep", "rep"), None, None),
        P("grp", ("rep", "seq")),
        P(None, "grp", ("rep", "seq"), None, "ep"),
        P("ep", "seq"),
        P(),
        P(("ep", "rep"), None, None, "seq"),
        P(("ep", "rep"), "seq", None),
        P(("grp", "ep", "rep"), None),
        P(("grp", "ep", "rep"), None),
    )
    return jax.shard_map(
        local, mesh=mesh, in_specs=placed, out_specs=P(("grp", "ep", "rep"), "seq"), check_vma=False
    )
```

```python
import functools
import math

import jax
import jax.numpy as jnp
from jax import lax
from jax.experimental import pallas as pl
from jax.experimental.pallas import tpu as pltpu
from jax.sharding import PartitionSpec as P

HEAD_DIM = 128
LANES = 128
PART = 8
ROWS = 32
VMEM_LIMIT = 50 << 20
epsilon = 1e-06
masked_score = -1e30


def attend_kernel(fresh_ref, len_ref, k_ref, v_ref, o_ref):
    rows, positions, width = k_ref.shape[1:]
    heads = width // HEAD_DIM
    part = math.gcd(rows, PART)
    parts = rows // part
    group = heads * part
    q, key_new, value_new = (fresh_ref[0, n].astype(jnp.float32) for n in range(3))
    score_scale = 1.0 / math.sqrt(HEAD_DIM)
    head_of = lax.broadcasted_iota(jnp.int32, (part, width), 1) // HEAD_DIM
    which = lax.broadcasted_iota(jnp.int32, (group, positions), 0) % part
    order = [(g, h) for g in range(parts) for h in range(heads)]

    def stacked(v):
        return jnp.concatenate(
            [
                v[g * part : (g + 1) * part, h * HEAD_DIM : (h + 1) * HEAD_DIM]
                for g, h in order
            ],
            axis=0,
        )

    own = jnp.sum(stacked(q * key_new), axis=1, keepdims=True) * score_scale
    pieces = []
    for g in range(parts):
        mine = q[g * part : (g + 1) * part]
        spread = jnp.concatenate(
            [jnp.where(head_of == h, mine, 0.0) for h in range(heads)], axis=0
        ).astype(jnp.bfloat16)
        keys = k_ref[0, g * part : (g + 1) * part].reshape(part * positions, width)
        every = lax.dot_general(
            spread, keys, (((1,), (1,)), ((), ())), preferred_element_type=jnp.float32
        )
        scores = every[:, :positions]
        for row in range(1, part):
            scores = jnp.where(
                which == row, every[:, row * positions : (row + 1) * positions], scores
            )
        pieces.append(scores)
    scores = jnp.concatenate(pieces, axis=0) * score_scale
    lengths = len_ref[...]
    lengths = jnp.concatenate([lengths[g * part : (g + 1) * part] for g, h in order], axis=0)
    in_cache = lax.broadcasted_iota(jnp.int32, scores.shape, 1) < lengths
    scores = jnp.where(in_cache, scores, masked_score)
    top = jnp.maximum(jnp.max(scores, axis=1, keepdims=True), own)
    weights = jnp.where(in_cache, jnp.exp(scores - top), 0.0)
    own_weight = jnp.exp(own - top)
    total = jnp.sum(weights, axis=1, keepdims=True) + own_weight
    added = own_weight * stacked(value_new)
    pieces = []
    for g in range(parts):
        mine = weights[g * group : (g + 1) * group]
        blocks = jnp.concatenate(
            [jnp.where(which == row, mine, 0.0).astype(jnp.bfloat16) for row in range(part)],
            axis=1,
        )
        values = v_ref[0, g * part : (g + 1) * part].reshape(part * positions, width)
        summed = lax.dot_general(
            blocks, values, (((1,), (0,)), ((), ())), preferred_element_type=jnp.float32
        )
        pieces += [
            summed[h * part : (h + 1) * part, h * HEAD_DIM : (h + 1) * HEAD_DIM]
            for h in range(heads)
        ]
    attended = (jnp.concatenate(pieces, axis=0) + added) / total
    attended = jnp.concatenate(
        [
            jnp.concatenate(
                [
                    attended[(g * heads + h) * part : (g * heads + h + 1) * part]
                    for h in range(heads)
                ],
                axis=1,
            )
            for g in range(parts)
        ],
        axis=0,
    )
    o_ref[...] = attended.astype(jnp.bfloat16)


def attend(fresh, lengths, kv):
    _, n, positions, width = kv.shape
    rows = fresh.shape[2]
    return pl.pallas_call(
        attend_kernel,
        grid=(n // rows,),
        in_specs=[
            pl.BlockSpec((1, 3, rows, width), lambda i: (i, 0, 0, 0)),
            pl.BlockSpec((rows, 1), lambda i: (i, 0)),
            pl.BlockSpec((1, rows, positions, width), lambda i: (0, i, 0, 0)),
            pl.BlockSpec((1, rows, positions, width), lambda i: (1, i, 0, 0)),
        ],
        out_specs=pl.BlockSpec((rows, width), lambda i: (i, 0)),
        out_shape=jax.ShapeDtypeStruct((n, width), jnp.bfloat16),
        compiler_params=pltpu.CompilerParams(vmem_limit_bytes=28 << 20),
        cost_estimate=pl.CostEstimate(
            flops=4 * n * positions * width,
            bytes_accessed=4 * n * positions * width,
            transcendentals=0,
        ),
    )(fresh, lengths, kv, kv)


def pieces_of(size, most):
    if size % LANES:
        return [(0, size)]
    return [(at, min(most, size - at)) for at in range(0, size, most)]


def expert_kernel(count, outs, mine_ref, *refs):
    slots, (w_ref, d_ref), y_refs = refs[:count], refs[count : count + 2], refs[count + 2 :][:outs]
    x_ref, c_ref, h_ref, in_ref, down_ref, in_sem, down_sem = refs[count + 2 + outs :]
    each = slots[0].shape[0]
    _, width, units = w_ref.shape
    in_cuts, down_cuts = pieces_of(units, 256), pieces_of(width, 512)
    in_copies, down_copies = [], []
    for n, (at, size) in enumerate(in_cuts):
        for half in range(2):
            src, dst = w_ref.at[half], in_ref.at[half]
            if size < units:
                src, dst = src.at[:, pl.ds(at, size)], dst.at[:, pl.ds(at, size)]
            in_copies.append(pltpu.make_async_copy(src, dst, in_sem.at[n, half]))
    for n, (at, size) in enumerate(down_cuts):
        down_copies.append(
            pltpu.make_async_copy(
                d_ref.at[:, pl.ds(at, size)], down_ref.at[:, pl.ds(at, size)], down_sem.at[n]
            )
        )
    for copy in in_copies + down_copies:
        copy.start()
    for n, slot in enumerate(slots):
        place = pl.ds(n * each, each)
        x_ref[place, :] = slot[:, :width]
        gates = slot[:, width:].astype(jnp.float32)
        lane = lax.broadcasted_iota(jnp.int32, gates.shape, 1)
        chosen = jnp.where(lane == mine_ref[0], gates, 0.0)
        c_ref[place, :] = jnp.sum(chosen, axis=1, keepdims=True)

    def keep(n, gate, up):
        at, size = in_cuts[n]
        h_ref[:, at : at + size] = (gate / (1.0 + jnp.exp(-gate)) * up).astype(jnp.bfloat16)

    def give(n, y):
        at, size = down_cuts[n]
        y = (y.astype(jnp.bfloat16).astype(jnp.float32) * c_ref[...]).astype(jnp.bfloat16)
        rows = y.shape[0] // outs
        for m, out in enumerate(y_refs):
            out[:, at : at + size] = y[m * rows : (m + 1) * rows]

    held = None
    for n, (at, size) in enumerate(in_cuts):
        in_copies[2 * n].wait()
        in_copies[2 * n + 1].wait()
        place = slice(at, at + size)
        gate = jnp.dot(x_ref[...], in_ref[0, :, place], preferred_element_type=jnp.float32)
        up = jnp.dot(x_ref[...], in_ref[1, :, place], preferred_element_type=jnp.float32)
        if held is not None:
            keep(*held)
        held = (n, gate, up)
    keep(*held)
    held = None
    for n, (at, size) in enumerate(down_cuts):
        down_copies[n].wait()
        place = slice(at, at + size)
        y = jnp.dot(h_ref[...], down_ref[:, place], preferred_element_type=jnp.float32)
        if held is not None:
            give(*held)
        held = (n, y)
    give(*held)


def expert(slots, outs, mine, w_both, w_down):
    each, packed = slots[0].shape
    rows = each * len(slots)
    _, depth, units = w_both.shape
    width = w_down.shape[1]
    inside = pl.BlockSpec(memory_space=pltpu.VMEM)
    return pl.pallas_call(
        functools.partial(expert_kernel, len(slots), outs),
        in_specs=[pl.BlockSpec(memory_space=pltpu.SMEM)]
        + [inside] * len(slots)
        + [pl.BlockSpec(memory_space=pl.ANY)] * 2,
        out_specs=[inside] * outs,
        scratch_shapes=[
            pltpu.VMEM((rows, depth), jnp.bfloat16),
            pltpu.VMEM((rows, 1), jnp.float32),
            pltpu.VMEM((rows, units), jnp.bfloat16),
            pltpu.VMEM((2, depth, units), jnp.bfloat16),
            pltpu.VMEM((units, width), jnp.bfloat16),
            pltpu.SemaphoreType.DMA((len(pieces_of(units, 256)), 2)),
            pltpu.SemaphoreType.DMA((len(pieces_of(width, 512)),)),
        ],
        out_shape=[jax.ShapeDtypeStruct((rows // outs, width), jnp.bfloat16)] * outs,
        compiler_params=pltpu.CompilerParams(vmem_limit_bytes=VMEM_LIMIT),
        cost_estimate=pl.CostEstimate(
            flops=6 * rows * depth * units,
            bytes_accessed=2 * (3 * depth * units + 2 * rows * depth),
            transcendentals=rows * units,
        ),
    )(mine, *slots, w_both, w_down)


def local(
    hidden_in,
    row_counts,
    qkv_new,
    cache_len,
    kv_cache,
    w_out,
    moe_gain,
    w_in,
    w_down,
    route_ids,
    route_weight,
):
    wide = jnp.float32
    narrow = jnp.bfloat16
    tok_rows, feat_local = hidden_in.shape
    owners = lax.axis_size("ep")
    reps = lax.axis_size("rep")
    parts_seq = lax.axis_size("seq")
    width_local = kv_cache.shape[-1]
    positions = kv_cache.shape[3]
    share_rows = tok_rows // parts_seq
    attend_rows = owners * share_rows
    inner = 2 if owners % 2 == 0 else 1
    outer = owners // inner
    me = lax.axis_index("ep")
    outer_me, inner_me = me // inner, me % inner

    def across(v):
        return lax.ppermute(v, "ep", [(i, i ^ 1) for i in range(owners)])

    def along(v, k):
        pairs = [
            (i, (i // inner + k) % outer * inner + i % inner) for i in range(owners)
        ]
        return lax.ppermute(v, "ep", pairs)

    def other(v):
        return lax.ppermute(v, "rep", [(i, (i + 1) % reps) for i in range(reps)])

    def rows_of_seq(v, axis):
        return lax.dynamic_slice_in_dim(v, lax.axis_index("seq") * share_rows, share_rows, axis)

    sent = qkv_new.reshape(tok_rows, 3, owners, width_local).transpose(2, 1, 0, 3)
    fresh = lax.all_to_all(sent, "ep", split_axis=0, concat_axis=0, tiled=True)
    fresh = rows_of_seq(fresh, 2)
    tile = math.gcd(attend_rows, ROWS)
    if share_rows != tile:
        fresh = fresh.transpose(0, 2, 1, 3).reshape(attend_rows // tile, tile, 3, width_local)
        fresh = fresh.transpose(0, 2, 1, 3)

    w_both = w_in.transpose(0, 2, 1, 3)
    if inner == 2 and reps == 2:
        half = w_out.shape[0] // 2
        rep_first = lax.axis_index("rep") == 0
        w_mine = jnp.where(rep_first, w_out[:half], w_out[half:])
    else:
        w_mine = w_out
    fresh, w_both, w_mine = lax.optimization_barrier((fresh, w_both, w_mine))
    w_mine = across(w_mine) if inner == 2 else w_mine

    kv = kv_cache.reshape(2, attend_rows, positions, width_local)
    attended = attend(fresh, cache_len.reshape(attend_rows, 1), kv)
    attended, w_mine = lax.optimization_barrier((attended, w_mine))
    attended = attended.reshape(owners, share_rows, width_local)
    attended = lax.all_gather(attended, "seq", axis=1, tiled=True)

    attended = attended.reshape(outer, inner, tok_rows, width_local)
    if inner == 2:
        first = inner_me == 0
        kept = jnp.where(first, attended[:, 0], attended[:, 1])
        given = jnp.where(first, attended[:, 1], attended[:, 0])
        joined = jnp.concatenate([kept, across(given)], axis=2)
        if reps == 2:
            theirs = other(w_mine)
            both = jnp.concatenate(
                [jnp.where(rep_first, w_mine, theirs), jnp.where(rep_first, theirs, w_mine)],
                axis=0,
            )
        else:
            both = w_mine
        w_pair = jnp.concatenate([w_out, both], axis=0)
    else:
        joined, w_pair = attended[:, 0], w_out
    turned = lax.dynamic_slice_in_dim(
        jnp.concatenate([joined, joined], axis=0), outer_me, outer, 0
    )
    partial_out = jnp.dot(
        turned.reshape(outer * tok_rows, -1), w_pair, preferred_element_type=wide
    ).reshape(outer, tok_rows, feat_local)
    arrived = [along(partial_out[k].astype(narrow), k) for k in range(1, outer)]
    attn_out = partial_out[0]
    for part in arrived:
        attn_out = attn_out + part.astype(wide)
    residual = (hidden_in.astype(wide) + attn_out).astype(narrow)
    residual_wide = residual.astype(wide)

    is_live = jnp.arange(tok_rows, dtype=jnp.int32) < row_counts[0]
    experts_local = w_in.shape[0]
    expert_total = owners * reps * experts_local
    hits = route_ids[:, :, None] == jnp.arange(expert_total, dtype=jnp.int32)[None, None, :]
    hits = hits & is_live[:, None, None]
    coeffs = jnp.sum(jnp.where(hits, route_weight.astype(wide)[:, :, None], 0.0), axis=1)
    lanes = -(-expert_total // LANES) * LANES
    coeffs = jnp.pad(coeffs, ((0, 0), (0, lanes - expert_total))).astype(narrow)
    full_rows = lax.all_gather(residual, "seq", axis=1, tiled=True).astype(wide)
    width = full_rows.shape[1]
    inverse_rms = lax.rsqrt(jnp.mean(full_rows * full_rows, axis=1) + epsilon)
    normed = (full_rows * inverse_rms[:, None] * moe_gain).astype(narrow)
    packed = jnp.concatenate([normed, coeffs], axis=1)
    columns = [packed, across(packed)] if inner == 2 else [packed]
    ks = list(range(outer))
    groups = [ks[: outer // 2], ks[outer // 2 :]] if outer > 1 else [ks]
    gathered = [[along(c, k) if k else c for c in columns for k in group] for group in groups]
    first_expert = (me * reps + lax.axis_index("rep")) * experts_local

    def run_experts(slots):
        if reps == 2:
            slots = slots + [other(s) for s in slots]
        total = None
        for j in range(experts_local):
            mine = jnp.reshape(first_expert + j, (1,)).astype(jnp.int32)
            made = expert(slots, reps, mine, w_both[j], w_down[j])
            total = made if total is None else [t + m for t, m in zip(total, made)]
        if parts_seq > 1:
            total = [
                lax.psum_scatter(t.astype(wide), "seq", scatter_dimension=1, tiled=True).astype(
                    narrow
                )
                for t in total
            ]
        return [t.reshape(inner, -1, tok_rows, feat_local) for t in total]

    def over_reps(made):
        merged = made[0].astype(wide)
        return merged + other(made[1]).astype(wide) if reps == 2 else merged

    cut = feat_local // 2

    def pair(v, k):
        return along(v.astype(narrow), -k).astype(wide)

    if len(groups) == 2 and inner == 2:
        made = run_experts(gathered[0])
        made, late = lax.optimization_barrier((made, gathered[1]))
        early = over_reps(made)
        early_parts = [
            along(early[:, i].astype(narrow), -k) for i, k in enumerate(groups[0]) if k
        ]
        made = run_experts(late)
        made, early_parts = lax.optimization_barrier((made, early_parts))
        late_sum = over_reps(made)
        base = early[:, 0]
        for part in early_parts:
            base = base + part.astype(wide)
        right_far = across(
            jnp.concatenate([late_sum[1, :, :, cut:], base[None, 1, :, cut:]]).astype(narrow)
        ).astype(wide)
        left = base[..., :cut]
        for i, k in enumerate(groups[1]):
            left = left + pair(late_sum[:, i, :, :cut], k)
        right = base[0, :, cut:] + right_far[-1]
        for i, k in enumerate(groups[1]):
            right = right + pair(late_sum[0, i, :, cut:] + right_far[i], k)
        left = left[0] + across(left[1].astype(narrow)).astype(wide)
        moe_out = jnp.concatenate([left, right], axis=1)
    else:
        total = jnp.zeros((inner, tok_rows, feat_local), wide)
        for group, slots in zip(groups, gathered):
            made = over_reps(run_experts(slots))
            for i, k in enumerate(group):
                total = total + (pair(made[:, i], k) if k else made[:, i])
        moe_out = total[0]
        if inner == 2:
            moe_out = moe_out + across(total[1].astype(narrow)).astype(wide)
    return jnp.where(is_live[:, None], residual_wide + moe_out, 0.0).astype(narrow)


def solution(mesh):
    placed = (
        P(("grp", "ep", "rep"), "seq"),
        P(("grp", "ep", "rep")),
        P(("grp", "ep", "rep"), None, None),
        P("grp", ("rep", "seq")),
        P(None, "grp", ("rep", "seq"), None, "ep"),
        P("ep", "seq"),
        P(),
        P(("ep", "rep"), None, None, "seq"),
        P(("ep", "rep"), "seq", None),
        P(("grp", "ep", "rep"), None),
        P(("grp", "ep", "rep"), None),
    )
    return jax.shard_map(
        local, mesh=mesh, in_specs=placed, out_specs=P(("grp", "ep", "rep"), "seq"), check_vma=False
    )
```

```python
import functools
import math

import jax
import jax.numpy as jnp
from jax import lax
from jax.experimental import pallas as pl
from jax.experimental.pallas import tpu as pltpu
from jax.sharding import PartitionSpec as P

HEAD_DIM = 128
LANES = 128
PART = 8
ROWS = 32
VMEM_LIMIT = 50 << 20
AHEAD = 4
epsilon = 1e-06
masked_score = -1e30


def attend_kernel(fresh_ref, len_ref, k_ref, v_ref, o_ref):
    rows, positions, width = k_ref.shape[1:]
    heads = width // HEAD_DIM
    part = math.gcd(rows, PART)
    parts = rows // part
    group = heads * part
    q, key_new, value_new = (fresh_ref[0, n].astype(jnp.float32) for n in range(3))
    score_scale = 1.0 / math.sqrt(HEAD_DIM)
    head_of = lax.broadcasted_iota(jnp.int32, (part, width), 1) // HEAD_DIM
    which = lax.broadcasted_iota(jnp.int32, (group, positions), 0) % part
    order = [(g, h) for g in range(parts) for h in range(heads)]

    def stacked(v):
        return jnp.concatenate(
            [
                v[g * part : (g + 1) * part, h * HEAD_DIM : (h + 1) * HEAD_DIM]
                for g, h in order
            ],
            axis=0,
        )

    own = jnp.sum(stacked(q * key_new), axis=1, keepdims=True) * score_scale
    pieces = []
    for g in range(parts):
        mine = q[g * part : (g + 1) * part]
        spread = jnp.concatenate(
            [jnp.where(head_of == h, mine, 0.0) for h in range(heads)], axis=0
        ).astype(jnp.bfloat16)
        keys = k_ref[0, g * part : (g + 1) * part].reshape(part * positions, width)
        every = lax.dot_general(
            spread, keys, (((1,), (1,)), ((), ())), preferred_element_type=jnp.float32
        )
        scores = every[:, :positions]
        for row in range(1, part):
            scores = jnp.where(
                which == row, every[:, row * positions : (row + 1) * positions], scores
            )
        pieces.append(scores)
    scores = jnp.concatenate(pieces, axis=0) * score_scale
    lengths = len_ref[...]
    lengths = jnp.concatenate([lengths[g * part : (g + 1) * part] for g, h in order], axis=0)
    in_cache = lax.broadcasted_iota(jnp.int32, scores.shape, 1) < lengths
    scores = jnp.where(in_cache, scores, masked_score)
    top = jnp.maximum(jnp.max(scores, axis=1, keepdims=True), own)
    weights = jnp.where(in_cache, jnp.exp(scores - top), 0.0)
    own_weight = jnp.exp(own - top)
    total = jnp.sum(weights, axis=1, keepdims=True) + own_weight
    added = own_weight * stacked(value_new)
    pieces = []
    for g in range(parts):
        mine = weights[g * group : (g + 1) * group]
        blocks = jnp.concatenate(
            [jnp.where(which == row, mine, 0.0).astype(jnp.bfloat16) for row in range(part)],
            axis=1,
        )
        values = v_ref[0, g * part : (g + 1) * part].reshape(part * positions, width)
        summed = lax.dot_general(
            blocks, values, (((1,), (0,)), ((), ())), preferred_element_type=jnp.float32
        )
        pieces += [
            summed[h * part : (h + 1) * part, h * HEAD_DIM : (h + 1) * HEAD_DIM]
            for h in range(heads)
        ]
    attended = (jnp.concatenate(pieces, axis=0) + added) / total
    attended = jnp.concatenate(
        [
            jnp.concatenate(
                [
                    attended[(g * heads + h) * part : (g * heads + h + 1) * part]
                    for h in range(heads)
                ],
                axis=1,
            )
            for g in range(parts)
        ],
        axis=0,
    )
    o_ref[...] = attended.astype(jnp.bfloat16)


def attend(fresh, lengths, kv):
    _, n, positions, width = kv.shape
    rows = fresh.shape[2]
    return pl.pallas_call(
        attend_kernel,
        grid=(n // rows,),
        in_specs=[
            pl.BlockSpec((1, 3, rows, width), lambda i: (i, 0, 0, 0)),
            pl.BlockSpec((rows, 1), lambda i: (i, 0)),
            pl.BlockSpec((1, rows, positions, width), lambda i: (0, i, 0, 0)),
            pl.BlockSpec((1, rows, positions, width), lambda i: (1, i, 0, 0)),
        ],
        out_specs=pl.BlockSpec((rows, width), lambda i: (i, 0)),
        out_shape=jax.ShapeDtypeStruct((n, width), jnp.bfloat16),
        compiler_params=pltpu.CompilerParams(vmem_limit_bytes=28 << 20),
        cost_estimate=pl.CostEstimate(
            flops=4 * n * positions * width,
            bytes_accessed=4 * n * positions * width,
            transcendentals=0,
        ),
    )(fresh, lengths, kv, kv)


def pieces_of(size, most):
    if size % LANES:
        return [(0, size)]
    return [(at, min(most, size - at)) for at in range(0, size, most)]


def expert_kernel(count, outs, mine_ref, *refs):
    slots, (w_ref, d_ref), y_refs = refs[:count], refs[count : count + 2], refs[count + 2 :][:outs]
    x_ref, c_ref, h_ref, in_ref, down_ref, in_sem, down_sem = refs[count + 2 + outs :]
    each = slots[0].shape[0]
    _, width, units = w_ref.shape
    in_cuts, down_cuts = pieces_of(units, 256), pieces_of(width, 512)
    in_copies, down_copies = [], []
    for n, (at, size) in enumerate(in_cuts):
        for half in range(2):
            src, dst = w_ref.at[half], in_ref.at[half]
            if size < units:
                src, dst = src.at[:, pl.ds(at, size)], dst.at[:, pl.ds(at, size)]
            in_copies.append(pltpu.make_async_copy(src, dst, in_sem.at[n, half]))
    for n, (at, size) in enumerate(down_cuts):
        down_copies.append(
            pltpu.make_async_copy(
                d_ref.at[:, pl.ds(at, size)], down_ref.at[:, pl.ds(at, size)], down_sem.at[n]
            )
        )
    copies = [in_copies[2 * n : 2 * n + 2] for n in range(len(in_cuts))]
    copies += [[copy] for copy in down_copies]

    def start(n):
        for copy in copies[n] if n < len(copies) else []:
            copy.start()

    for n in range(AHEAD):
        start(n)
    for n, slot in enumerate(slots):
        place = pl.ds(n * each, each)
        x_ref[place, :] = slot[:, :width]
        gates = slot[:, width:].astype(jnp.float32)
        lane = lax.broadcasted_iota(jnp.int32, gates.shape, 1)
        chosen = jnp.where(lane == mine_ref[0], gates, 0.0)
        c_ref[place, :] = jnp.sum(chosen, axis=1, keepdims=True)

    def keep(n, gate, up):
        at, size = in_cuts[n]
        h_ref[:, at : at + size] = (gate / (1.0 + jnp.exp(-gate)) * up).astype(jnp.bfloat16)

    def give(n, y):
        at, size = down_cuts[n]
        y = (y.astype(jnp.bfloat16).astype(jnp.float32) * c_ref[...]).astype(jnp.bfloat16)
        rows = y.shape[0] // outs
        for m, out in enumerate(y_refs):
            out[:, at : at + size] = y[m * rows : (m + 1) * rows]

    held = None
    for n, (at, size) in enumerate(in_cuts):
        start(n + AHEAD)
        in_copies[2 * n].wait()
        in_copies[2 * n + 1].wait()
        place = slice(at, at + size)
        gate = jnp.dot(x_ref[...], in_ref[0, :, place], preferred_element_type=jnp.float32)
        up = jnp.dot(x_ref[...], in_ref[1, :, place], preferred_element_type=jnp.float32)
        if held is not None:
            keep(*held)
        held = (n, gate, up)
    keep(*held)
    held = None
    for n, (at, size) in enumerate(down_cuts):
        start(len(in_cuts) + n + AHEAD)
        down_copies[n].wait()
        place = slice(at, at + size)
        y = jnp.dot(h_ref[...], down_ref[:, place], preferred_element_type=jnp.float32)
        if held is not None:
            give(*held)
        held = (n, y)
    give(*held)


def expert(slots, outs, mine, w_both, w_down):
    each, packed = slots[0].shape
    rows = each * len(slots)
    _, depth, units = w_both.shape
    width = w_down.shape[1]
    inside = pl.BlockSpec(memory_space=pltpu.VMEM)
    return pl.pallas_call(
        functools.partial(expert_kernel, len(slots), outs),
        in_specs=[pl.BlockSpec(memory_space=pltpu.SMEM)]
        + [inside] * len(slots)
        + [pl.BlockSpec(memory_space=pl.ANY)] * 2,
        out_specs=[inside] * outs,
        scratch_shapes=[
            pltpu.VMEM((rows, depth), jnp.bfloat16),
            pltpu.VMEM((rows, 1), jnp.float32),
            pltpu.VMEM((rows, units), jnp.bfloat16),
            pltpu.VMEM((2, depth, units), jnp.bfloat16),
            pltpu.VMEM((units, width), jnp.bfloat16),
            pltpu.SemaphoreType.DMA((len(pieces_of(units, 256)), 2)),
            pltpu.SemaphoreType.DMA((len(pieces_of(width, 512)),)),
        ],
        out_shape=[jax.ShapeDtypeStruct((rows // outs, width), jnp.bfloat16)] * outs,
        compiler_params=pltpu.CompilerParams(vmem_limit_bytes=VMEM_LIMIT),
        cost_estimate=pl.CostEstimate(
            flops=6 * rows * depth * units,
            bytes_accessed=2 * (3 * depth * units + 2 * rows * depth),
            transcendentals=rows * units,
        ),
    )(mine, *slots, w_both, w_down)


def local(
    hidden_in,
    row_counts,
    qkv_new,
    cache_len,
    kv_cache,
    w_out,
    moe_gain,
    w_in,
    w_down,
    route_ids,
    route_weight,
):
    wide = jnp.float32
    narrow = jnp.bfloat16
    tok_rows, feat_local = hidden_in.shape
    owners = lax.axis_size("ep")
    reps = lax.axis_size("rep")
    parts_seq = lax.axis_size("seq")
    width_local = kv_cache.shape[-1]
    positions = kv_cache.shape[3]
    share_rows = tok_rows // parts_seq
    attend_rows = owners * share_rows
    inner = 2 if owners % 2 == 0 else 1
    outer = owners // inner
    me = lax.axis_index("ep")
    outer_me, inner_me = me // inner, me % inner

    def across(v):
        return lax.ppermute(v, "ep", [(i, i ^ 1) for i in range(owners)])

    def along(v, k):
        pairs = [
            (i, (i // inner + k) % outer * inner + i % inner) for i in range(owners)
        ]
        return lax.ppermute(v, "ep", pairs)

    def other(v):
        return lax.ppermute(v, "rep", [(i, (i + 1) % reps) for i in range(reps)])

    def fence(*values):
        return lax.optimization_barrier(values)

    def rows_of_seq(v, axis):
        return lax.dynamic_slice_in_dim(v, lax.axis_index("seq") * share_rows, share_rows, axis)

    sent = qkv_new.reshape(tok_rows, 3, owners, width_local).transpose(2, 1, 0, 3)
    fresh = lax.all_to_all(sent, "ep", split_axis=0, concat_axis=0, tiled=True)
    fresh = rows_of_seq(fresh, 2)
    tile = math.gcd(attend_rows, ROWS)
    if share_rows != tile:
        fresh = fresh.transpose(0, 2, 1, 3).reshape(attend_rows // tile, tile, 3, width_local)
        fresh = fresh.transpose(0, 2, 1, 3)

    w_both = w_in.transpose(0, 2, 1, 3)
    if inner == 2 and reps == 2:
        half = w_out.shape[0] // 2
        rep_first = lax.axis_index("rep") == 0
        w_mine = jnp.where(rep_first, w_out[:half], w_out[half:])
    else:
        w_mine = w_out
    fresh, w_both, w_mine = lax.optimization_barrier((fresh, w_both, w_mine))
    w_mine = across(w_mine) if inner == 2 else w_mine

    kv = kv_cache.reshape(2, attend_rows, positions, width_local)
    attended = attend(fresh, cache_len.reshape(attend_rows, 1), kv)
    attended, w_mine = lax.optimization_barrier((attended, w_mine))
    attended = attended.reshape(owners, share_rows, width_local)
    attended = lax.all_gather(attended, "seq", axis=1, tiled=True)

    attended = attended.reshape(outer, inner, tok_rows, width_local)
    if inner == 2:
        first = inner_me == 0
        kept = jnp.where(first, attended[:, 0], attended[:, 1])
        given = jnp.where(first, attended[:, 1], attended[:, 0])
        joined = jnp.concatenate([kept, across(given)], axis=2)
        if reps == 2:
            theirs = other(w_mine)
            both = jnp.concatenate(
                [jnp.where(rep_first, w_mine, theirs), jnp.where(rep_first, theirs, w_mine)],
                axis=0,
            )
        else:
            both = w_mine
        w_pair = jnp.concatenate([w_out, both], axis=0)
    else:
        joined, w_pair = attended[:, 0], w_out
    turned = lax.dynamic_slice_in_dim(
        jnp.concatenate([joined, joined], axis=0), outer_me, outer, 0
    )
    partial_out = jnp.dot(
        turned.reshape(outer * tok_rows, -1), w_pair, preferred_element_type=wide
    ).reshape(outer, tok_rows, feat_local)
    arrived = [along(partial_out[k].astype(narrow), k) for k in range(1, outer)]
    attn_out = partial_out[0]
    for part in arrived:
        attn_out = attn_out + part.astype(wide)
    residual = (hidden_in.astype(wide) + attn_out).astype(narrow)
    residual_wide = residual.astype(wide)

    is_live = jnp.arange(tok_rows, dtype=jnp.int32) < row_counts[0]
    experts_local = w_in.shape[0]
    expert_total = owners * reps * experts_local
    hits = route_ids[:, :, None] == jnp.arange(expert_total, dtype=jnp.int32)[None, None, :]
    hits = hits & is_live[:, None, None]
    coeffs = jnp.sum(jnp.where(hits, route_weight.astype(wide)[:, :, None], 0.0), axis=1)
    lanes = -(-expert_total // LANES) * LANES
    coeffs = jnp.pad(coeffs, ((0, 0), (0, lanes - expert_total))).astype(narrow)
    full_rows = lax.all_gather(residual, "seq", axis=1, tiled=True).astype(wide)
    width = full_rows.shape[1]
    inverse_rms = lax.rsqrt(jnp.mean(full_rows * full_rows, axis=1) + epsilon)
    normed = (full_rows * inverse_rms[:, None] * moe_gain).astype(narrow)
    packed = jnp.concatenate([normed, coeffs], axis=1)
    near = [packed] + [along(packed, k) for k in range(1, outer)]
    far = []
    if inner == 2:
        middle = outer // 2
        far = [across(v) for k, v in enumerate(near) if k != middle or outer == 1]
        if outer > 1:
            *far, near[middle] = fence(*far, near[middle])
            far.insert(middle, across(near[middle]))
    first_expert = (me * reps + lax.axis_index("rep")) * experts_local

    def run_experts(slots):
        if reps == 2:
            slots = slots + [other(s) for s in slots]
        total = None
        for j in range(experts_local):
            mine = jnp.reshape(first_expert + j, (1,)).astype(jnp.int32)
            made = expert(slots, reps, mine, w_both[j], w_down[j])
            total = made if total is None else [t + m for t, m in zip(total, made)]
        if parts_seq > 1:
            total = [
                lax.psum_scatter(t.astype(wide), "seq", scatter_dimension=1, tiled=True).astype(
                    narrow
                )
                for t in total
            ]
        return [t.reshape(outer, tok_rows, feat_local) for t in total]

    def back(v):
        return [along(v[k].astype(narrow), -k) for k in range(1, outer)]

    def summed(first, parts):
        for part in parts:
            first = first + part.astype(wide)
        return first

    made = run_experts(near)
    if inner == 2:
        made, far = fence(made, far)
        swapped = [other(v) for v in made[1:]]
        far_made = run_experts(far)
        far_made, swapped = fence(far_made, swapped)
        far_sum = summed(far_made[0].astype(wide), [other(v) for v in far_made[1:]])
        near_sum = summed(made[0].astype(wide), swapped)
        moe_out, moe_far = near_sum[0], far_sum[0]
        inside = [outer // 2] + [k for k in range(1, outer - 1) if k != outer // 2]
        given = {k: across(far_sum[k].astype(narrow)) for k in inside if outer > 2}
        if outer > 1:
            last = jnp.stack([near_sum[-1], far_sum[-1]]).astype(narrow)
            last = along(last, 1 - outer).astype(wide)
            moe_out, moe_far = moe_out + last[0], moe_far + last[1]
        for k, part in given.items():
            part = near_sum[k] + part.astype(wide)
            moe_out = moe_out + along(part.astype(narrow), -k).astype(wide)
        moe_out = moe_out + across(moe_far.astype(narrow)).astype(wide)
    else:
        near_sum = summed(made[0].astype(wide), [other(v) for v in made[1:]])
        moe_out = summed(near_sum[0], back(near_sum))
    return jnp.where(is_live[:, None], residual_wide + moe_out, 0.0).astype(narrow)


def solution(mesh):
    placed = (
        P(("grp", "ep", "rep"), "seq"),
        P(("grp", "ep", "rep")),
        P(("grp", "ep", "rep"), None, None),
        P("grp", ("rep", "seq")),
        P(None, "grp", ("rep", "seq"), None, "ep"),
        P("ep", "seq"),
        P(),
        P(("ep", "rep"), None, None, "seq"),
        P(("ep", "rep"), "seq", None),
        P(("grp", "ep", "rep"), None),
        P(("grp", "ep", "rep"), None),
    )
    return jax.shard_map(
        local, mesh=mesh, in_specs=placed, out_specs=P(("grp", "ep", "rep"), "seq"), check_vma=False
    )
```

```python
import functools
import math

import jax
import jax.numpy as jnp
from jax import lax
from jax.experimental import pallas as pl
from jax.experimental.pallas import tpu as pltpu
from jax.sharding import PartitionSpec as P

HEAD_DIM = 128
LANES = 128
PART = 8
ROWS = 32
VMEM_LIMIT = 50 << 20
AHEAD = 4
epsilon = 1e-06
masked_score = -1e30


def attend_kernel(fresh_ref, len_ref, kv_ref, o_ref, near_ref, arrived):
    steps, _, rows, width = fresh_ref.shape
    positions = kv_ref.shape[2]

    def copies(step):
        place = pl.ds(pl.multiple_of(step * rows, rows), rows)
        return [
            pltpu.make_async_copy(
                kv_ref.at[n, place], near_ref.at[n, place], arrived.at[step, n]
            )
            for n in range(2)
        ]

    def start(step):
        for copy in copies(step):
            copy.start()

    for step in range(min(AHEAD, steps)):
        start(step)

    @pl.loop(0, steps)
    def _(step):
        @pl.when(step + AHEAD < steps)
        def _():
            start(step + AHEAD)

        keys, values = copies(step)
        attend_rows(step, fresh_ref, len_ref, near_ref, o_ref, keys.wait, values.wait)


def attend_rows(step, fresh_ref, len_ref, near_ref, o_ref, keys_arrive, values_arrive):
    rows, width = fresh_ref.shape[2:]
    positions = near_ref.shape[2]
    heads = width // HEAD_DIM
    part = math.gcd(rows, PART)
    parts = rows // part
    group = heads * part
    base = pl.multiple_of(step * rows, rows)
    q, key_new, value_new = (fresh_ref[step, n].astype(jnp.float32) for n in range(3))
    score_scale = 1.0 / math.sqrt(HEAD_DIM)
    head_of = lax.broadcasted_iota(jnp.int32, (part, width), 1) // HEAD_DIM
    which = lax.broadcasted_iota(jnp.int32, (group, positions), 0) % part
    order = [(g, h) for g in range(parts) for h in range(heads)]

    def stacked(v):
        return jnp.concatenate(
            [
                v[g * part : (g + 1) * part, h * HEAD_DIM : (h + 1) * HEAD_DIM]
                for g, h in order
            ],
            axis=0,
        )

    own = jnp.sum(stacked(q * key_new), axis=1, keepdims=True) * score_scale
    keys_arrive()
    pieces = []
    for g in range(parts):
        mine = q[g * part : (g + 1) * part]
        spread = jnp.concatenate(
            [jnp.where(head_of == h, mine, 0.0) for h in range(heads)], axis=0
        ).astype(jnp.bfloat16)
        keys = near_ref[0, pl.ds(base + g * part, part)].reshape(part * positions, width)
        every = lax.dot_general(
            spread, keys, (((1,), (1,)), ((), ())), preferred_element_type=jnp.float32
        )
        scores = every[:, :positions]
        for row in range(1, part):
            scores = jnp.where(
                which == row, every[:, row * positions : (row + 1) * positions], scores
            )
        pieces.append(scores)
    scores = jnp.concatenate(pieces, axis=0) * score_scale
    mine = jnp.broadcast_to(len_ref[pl.ds(step, 1), :], (rows, rows))
    diagonal = lax.broadcasted_iota(jnp.int32, (rows, rows), 0) == lax.broadcasted_iota(
        jnp.int32, (rows, rows), 1
    )
    lengths = jnp.sum(jnp.where(diagonal, mine, 0), axis=1, keepdims=True)
    lengths = jnp.concatenate([lengths[g * part : (g + 1) * part] for g, h in order], axis=0)
    in_cache = lax.broadcasted_iota(jnp.int32, scores.shape, 1) < lengths
    scores = jnp.where(in_cache, scores, masked_score)
    top = jnp.maximum(jnp.max(scores, axis=1, keepdims=True), own)
    weights = jnp.where(in_cache, jnp.exp(scores - top), 0.0)
    own_weight = jnp.exp(own - top)
    total = jnp.sum(weights, axis=1, keepdims=True) + own_weight
    added = own_weight * stacked(value_new)
    values_arrive()
    pieces = []
    for g in range(parts):
        mine = weights[g * group : (g + 1) * group]
        blocks = jnp.concatenate(
            [jnp.where(which == row, mine, 0.0).astype(jnp.bfloat16) for row in range(part)],
            axis=1,
        )
        values = near_ref[1, pl.ds(base + g * part, part)].reshape(part * positions, width)
        summed = lax.dot_general(
            blocks, values, (((1,), (0,)), ((), ())), preferred_element_type=jnp.float32
        )
        pieces += [
            summed[h * part : (h + 1) * part, h * HEAD_DIM : (h + 1) * HEAD_DIM]
            for h in range(heads)
        ]
    attended = (jnp.concatenate(pieces, axis=0) + added) / total
    attended = jnp.concatenate(
        [
            jnp.concatenate(
                [
                    attended[(g * heads + h) * part : (g * heads + h + 1) * part]
                    for h in range(heads)
                ],
                axis=1,
            )
            for g in range(parts)
        ],
        axis=0,
    )
    o_ref[pl.ds(base, rows), :] = attended.astype(jnp.bfloat16)


def attend(fresh, lengths, kv):
    _, n, positions, width = kv.shape
    steps = fresh.shape[0]
    inside = pl.BlockSpec(memory_space=pltpu.VMEM)
    return pl.pallas_call(
        attend_kernel,
        in_specs=[inside, inside, pl.BlockSpec(memory_space=pl.ANY)],
        out_specs=inside,
        out_shape=jax.ShapeDtypeStruct((n, width), jnp.bfloat16),
        scratch_shapes=[
            pltpu.VMEM(kv.shape, kv.dtype),
            pltpu.SemaphoreType.DMA((steps, 2)),
        ],
        compiler_params=pltpu.CompilerParams(vmem_limit_bytes=VMEM_LIMIT),
        cost_estimate=pl.CostEstimate(
            flops=4 * n * positions * width,
            bytes_accessed=4 * n * positions * width,
            transcendentals=0,
        ),
    )(fresh, lengths, kv)


def pieces_of(size, most):
    if size % LANES:
        return [(0, size)]
    return [(at, min(most, size - at)) for at in range(0, size, most)]


def expert_kernel(count, outs, mine_ref, *refs):
    slots, (w_ref, d_ref), y_refs = refs[:count], refs[count : count + 2], refs[count + 2 :][:outs]
    x_ref, c_ref, h_ref, in_ref, down_ref, in_sem, down_sem = refs[count + 2 + outs :]
    each = slots[0].shape[0]
    _, width, units = w_ref.shape
    in_cuts, down_cuts = pieces_of(units, 256), pieces_of(width, 512)
    in_copies, down_copies = [], []
    for n, (at, size) in enumerate(in_cuts):
        for half in range(2):
            src, dst = w_ref.at[half], in_ref.at[half]
            if size < units:
                src, dst = src.at[:, pl.ds(at, size)], dst.at[:, pl.ds(at, size)]
            in_copies.append(pltpu.make_async_copy(src, dst, in_sem.at[n, half]))
    for n, (at, size) in enumerate(down_cuts):
        down_copies.append(
            pltpu.make_async_copy(
                d_ref.at[:, pl.ds(at, size)], down_ref.at[:, pl.ds(at, size)], down_sem.at[n]
            )
        )
    copies = [in_copies[2 * n : 2 * n + 2] for n in range(len(in_cuts))]
    copies += [[copy] for copy in down_copies]

    def start(n):
        for copy in copies[n] if n < len(copies) else []:
            copy.start()

    for n in range(AHEAD):
        start(n)
    for n, slot in enumerate(slots):
        place = pl.ds(n * each, each)
        x_ref[place, :] = slot[:, :width]
        gates = slot[:, width:].astype(jnp.float32)
        lane = lax.broadcasted_iota(jnp.int32, gates.shape, 1)
        chosen = jnp.where(lane == mine_ref[0], gates, 0.0)
        c_ref[place, :] = jnp.sum(chosen, axis=1, keepdims=True)

    def keep(n, gate, up):
        at, size = in_cuts[n]
        h_ref[:, at : at + size] = (gate / (1.0 + jnp.exp(-gate)) * up).astype(jnp.bfloat16)

    def give(n, y):
        at, size = down_cuts[n]
        y = (y.astype(jnp.bfloat16).astype(jnp.float32) * c_ref[...]).astype(jnp.bfloat16)
        rows = y.shape[0] // outs
        for m, out in enumerate(y_refs):
            out[:, at : at + size] = y[m * rows : (m + 1) * rows]

    held = None
    for n, (at, size) in enumerate(in_cuts):
        start(n + AHEAD)
        in_copies[2 * n].wait()
        in_copies[2 * n + 1].wait()
        place = slice(at, at + size)
        gate = jnp.dot(x_ref[...], in_ref[0, :, place], preferred_element_type=jnp.float32)
        up = jnp.dot(x_ref[...], in_ref[1, :, place], preferred_element_type=jnp.float32)
        if held is not None:
            keep(*held)
        held = (n, gate, up)
    keep(*held)
    held = None
    for n, (at, size) in enumerate(down_cuts):
        start(len(in_cuts) + n + AHEAD)
        down_copies[n].wait()
        place = slice(at, at + size)
        y = jnp.dot(h_ref[...], down_ref[:, place], preferred_element_type=jnp.float32)
        if held is not None:
            give(*held)
        held = (n, y)
    give(*held)


def expert(slots, outs, mine, w_both, w_down):
    each, packed = slots[0].shape
    rows = each * len(slots)
    _, depth, units = w_both.shape
    width = w_down.shape[1]
    inside = pl.BlockSpec(memory_space=pltpu.VMEM)
    return pl.pallas_call(
        functools.partial(expert_kernel, len(slots), outs),
        in_specs=[pl.BlockSpec(memory_space=pltpu.SMEM)]
        + [inside] * len(slots)
        + [pl.BlockSpec(memory_space=pl.ANY)] * 2,
        out_specs=[inside] * outs,
        scratch_shapes=[
            pltpu.VMEM((rows, depth), jnp.bfloat16),
            pltpu.VMEM((rows, 1), jnp.float32),
            pltpu.VMEM((rows, units), jnp.bfloat16),
            pltpu.VMEM((2, depth, units), jnp.bfloat16),
            pltpu.VMEM((units, width), jnp.bfloat16),
            pltpu.SemaphoreType.DMA((len(pieces_of(units, 256)), 2)),
            pltpu.SemaphoreType.DMA((len(pieces_of(width, 512)),)),
        ],
        out_shape=[jax.ShapeDtypeStruct((rows // outs, width), jnp.bfloat16)] * outs,
        compiler_params=pltpu.CompilerParams(vmem_limit_bytes=VMEM_LIMIT),
        cost_estimate=pl.CostEstimate(
            flops=6 * rows * depth * units,
            bytes_accessed=2 * (3 * depth * units + 2 * rows * depth),
            transcendentals=rows * units,
        ),
    )(mine, *slots, w_both, w_down)


def local(
    hidden_in,
    row_counts,
    qkv_new,
    cache_len,
    kv_cache,
    w_out,
    moe_gain,
    w_in,
    w_down,
    route_ids,
    route_weight,
):
    wide = jnp.float32
    narrow = jnp.bfloat16
    tok_rows, feat_local = hidden_in.shape
    owners = lax.axis_size("ep")
    reps = lax.axis_size("rep")
    parts_seq = lax.axis_size("seq")
    width_local = kv_cache.shape[-1]
    positions = kv_cache.shape[3]
    share_rows = tok_rows // parts_seq
    attend_rows = owners * share_rows
    inner = 2 if owners % 2 == 0 else 1
    outer = owners // inner
    me = lax.axis_index("ep")
    outer_me, inner_me = me // inner, me % inner

    def across(v):
        return lax.ppermute(v, "ep", [(i, i ^ 1) for i in range(owners)])

    def along(v, k):
        pairs = [
            (i, (i // inner + k) % outer * inner + i % inner) for i in range(owners)
        ]
        return lax.ppermute(v, "ep", pairs)

    def other(v):
        return lax.ppermute(v, "rep", [(i, (i + 1) % reps) for i in range(reps)])

    def fence(*values):
        return lax.optimization_barrier(values)

    def rows_of_seq(v, axis):
        return lax.dynamic_slice_in_dim(v, lax.axis_index("seq") * share_rows, share_rows, axis)

    sent = qkv_new.reshape(tok_rows, 3, owners, width_local).transpose(2, 1, 0, 3)
    fresh = lax.all_to_all(sent, "ep", split_axis=0, concat_axis=0, tiled=True)
    fresh = rows_of_seq(fresh, 2)
    tile = math.gcd(attend_rows, ROWS)
    if share_rows != tile:
        fresh = fresh.transpose(0, 2, 1, 3).reshape(attend_rows // tile, tile, 3, width_local)
        fresh = fresh.transpose(0, 2, 1, 3)

    w_both = w_in.transpose(0, 2, 1, 3)
    if inner == 2 and reps == 2:
        half = w_out.shape[0] // 2
        rep_first = lax.axis_index("rep") == 0
        w_mine = jnp.where(rep_first, w_out[:half], w_out[half:])
    else:
        w_mine = w_out
    fresh, w_both, w_mine = fence(fresh, w_both, w_mine)
    w_mine = across(w_mine) if inner == 2 else w_mine

    kv = kv_cache.reshape(2, attend_rows, positions, width_local)
    attended = attend(fresh, cache_len.reshape(attend_rows // tile, tile), kv)
    attended, w_mine = lax.optimization_barrier((attended, w_mine))
    attended = attended.reshape(owners, share_rows, width_local)
    attended = lax.all_gather(attended, "seq", axis=1, tiled=True)

    attended = attended.reshape(outer, inner, tok_rows, width_local)
    if inner == 2:
        first = inner_me == 0
        kept = jnp.where(first, attended[:, 0], attended[:, 1])
        given = jnp.where(first, attended[:, 1], attended[:, 0])
        joined = jnp.concatenate([kept, across(given)], axis=2)
        if reps == 2:
            theirs = other(w_mine)
            both = jnp.concatenate(
                [jnp.where(rep_first, w_mine, theirs), jnp.where(rep_first, theirs, w_mine)],
                axis=0,
            )
        else:
            both = w_mine
        w_pair = jnp.concatenate([w_out, both], axis=0)
    else:
        joined, w_pair = attended[:, 0], w_out
    turned = lax.dynamic_slice_in_dim(
        jnp.concatenate([joined, joined], axis=0), outer_me, outer, 0
    )
    partial_out = jnp.dot(
        turned.reshape(outer * tok_rows, -1), w_pair, preferred_element_type=wide
    ).reshape(outer, tok_rows, feat_local)
    arrived = [along(partial_out[k].astype(narrow), k) for k in range(1, outer)]
    attn_out = partial_out[0]
    for part in arrived:
        attn_out = attn_out + part.astype(wide)
    residual = (hidden_in.astype(wide) + attn_out).astype(narrow)
    residual_wide = residual.astype(wide)

    is_live = jnp.arange(tok_rows, dtype=jnp.int32) < row_counts[0]
    experts_local = w_in.shape[0]
    expert_total = owners * reps * experts_local
    hits = route_ids[:, :, None] == jnp.arange(expert_total, dtype=jnp.int32)[None, None, :]
    hits = hits & is_live[:, None, None]
    coeffs = jnp.sum(jnp.where(hits, route_weight.astype(wide)[:, :, None], 0.0), axis=1)
    lanes = -(-expert_total // LANES) * LANES
    coeffs = jnp.pad(coeffs, ((0, 0), (0, lanes - expert_total))).astype(narrow)
    full_rows = lax.all_gather(residual, "seq", axis=1, tiled=True).astype(wide)
    width = full_rows.shape[1]
    inverse_rms = lax.rsqrt(jnp.mean(full_rows * full_rows, axis=1) + epsilon)
    normed = (full_rows * inverse_rms[:, None] * moe_gain).astype(narrow)
    packed = jnp.concatenate([normed, coeffs], axis=1)
    near = [packed] + [along(packed, k) for k in range(1, outer)]
    far = []
    if inner == 2:
        middle = outer // 2
        far = [across(v) for k, v in enumerate(near) if k != middle or outer == 1]
        if outer > 1:
            *far, near[middle] = fence(*far, near[middle])
            far.insert(middle, across(near[middle]))
    first_expert = (me * reps + lax.axis_index("rep")) * experts_local

    def run_experts(slots):
        if reps == 2:
            slots = slots + [other(s) for s in slots]
        total = None
        for j in range(experts_local):
            mine = jnp.reshape(first_expert + j, (1,)).astype(jnp.int32)
            made = expert(slots, reps, mine, w_both[j], w_down[j])
            total = made if total is None else [t + m for t, m in zip(total, made)]
        if parts_seq > 1:
            total = [
                lax.psum_scatter(t.astype(wide), "seq", scatter_dimension=1, tiled=True).astype(
                    narrow
                )
                for t in total
            ]
        return [t.reshape(outer, tok_rows, feat_local) for t in total]

    def back(v):
        return [along(v[k].astype(narrow), -k) for k in range(1, outer)]

    def summed(first, parts):
        for part in parts:
            first = first + part.astype(wide)
        return first

    made = run_experts(near)
    if inner == 2:
        made, far = fence(made, far)
        swapped = [other(v) for v in made[1:]]
        far_made = run_experts(far)
        far_made, swapped = fence(far_made, swapped)
        far_sum = summed(far_made[0].astype(wide), [other(v) for v in far_made[1:]])
        near_sum = summed(made[0].astype(wide), swapped)
        moe_out, moe_far = near_sum[0], far_sum[0]
        inside = [outer // 2] + [k for k in range(1, outer - 1) if k != outer // 2]
        given = {k: across(far_sum[k].astype(narrow)) for k in inside if outer > 2}
        if outer > 1:
            last = jnp.stack([near_sum[-1], far_sum[-1]]).astype(narrow)
            last = along(last, 1 - outer).astype(wide)
            moe_out, moe_far = moe_out + last[0], moe_far + last[1]
        for k, part in given.items():
            part = near_sum[k] + part.astype(wide)
            moe_out = moe_out + along(part.astype(narrow), -k).astype(wide)
        moe_out = moe_out + across(moe_far.astype(narrow)).astype(wide)
    else:
        near_sum = summed(made[0].astype(wide), [other(v) for v in made[1:]])
        moe_out = summed(near_sum[0], back(near_sum))
    return jnp.where(is_live[:, None], residual_wide + moe_out, 0.0).astype(narrow)


def solution(mesh):
    placed = (
        P(("grp", "ep", "rep"), "seq"),
        P(("grp", "ep", "rep")),
        P(("grp", "ep", "rep"), None, None),
        P("grp", ("rep", "seq")),
        P(None, "grp", ("rep", "seq"), None, "ep"),
        P("ep", "seq"),
        P(),
        P(("ep", "rep"), None, None, "seq"),
        P(("ep", "rep"), "seq", None),
        P(("grp", "ep", "rep"), None),
        P(("grp", "ep", "rep"), None),
    )
    return jax.shard_map(
        local, mesh=mesh, in_specs=placed, out_specs=P(("grp", "ep", "rep"), "seq"), check_vma=False
    )
```

```python
import functools
import math

import jax
import jax.numpy as jnp
from jax import lax
from jax.experimental import pallas as pl
from jax.experimental.pallas import tpu as pltpu
from jax.sharding import PartitionSpec as P

HEAD_DIM = 128
LANES = 128
PART = 8
ROWS = 32
VMEM_LIMIT = 50 << 20
AHEAD = 4
epsilon = 1e-06
masked_score = -1e30


def attend_kernel(fresh_ref, len_ref, kv_ref, o_ref, near_ref, arrived):
    steps, _, rows, width = fresh_ref.shape
    positions = kv_ref.shape[2]

    def copies(step):
        place = pl.ds(pl.multiple_of(step * rows, rows), rows)
        return [
            pltpu.make_async_copy(
                kv_ref.at[n, place], near_ref.at[n, place], arrived.at[step, n]
            )
            for n in range(2)
        ]

    def start(step):
        for copy in copies(step):
            copy.start()

    for step in range(min(AHEAD, steps)):
        start(step)

    @pl.loop(0, steps)
    def _(step):
        @pl.when(step + AHEAD < steps)
        def _():
            start(step + AHEAD)

        keys, values = copies(step)
        attend_rows(step, fresh_ref, len_ref, near_ref, o_ref, keys.wait, values.wait)


def attend_rows(step, fresh_ref, len_ref, near_ref, o_ref, keys_arrive, values_arrive):
    rows, width = fresh_ref.shape[2:]
    positions = near_ref.shape[2]
    heads = width // HEAD_DIM
    part = math.gcd(rows, PART)
    parts = rows // part
    group = heads * part
    base = pl.multiple_of(step * rows, rows)
    q, key_new, value_new = (fresh_ref[step, n].astype(jnp.float32) for n in range(3))
    score_scale = 1.0 / math.sqrt(HEAD_DIM)
    head_of = lax.broadcasted_iota(jnp.int32, (part, width), 1) // HEAD_DIM
    which = lax.broadcasted_iota(jnp.int32, (group, positions), 0) % part
    order = [(g, h) for g in range(parts) for h in range(heads)]

    def stacked(v):
        return jnp.concatenate(
            [
                v[g * part : (g + 1) * part, h * HEAD_DIM : (h + 1) * HEAD_DIM]
                for g, h in order
            ],
            axis=0,
        )

    own = jnp.sum(stacked(q * key_new), axis=1, keepdims=True) * score_scale
    keys_arrive()
    pieces = []
    for g in range(parts):
        mine = q[g * part : (g + 1) * part]
        spread = jnp.concatenate(
            [jnp.where(head_of == h, mine, 0.0) for h in range(heads)], axis=0
        ).astype(jnp.bfloat16)
        keys = near_ref[0, pl.ds(base + g * part, part)].reshape(part * positions, width)
        every = lax.dot_general(
            spread, keys, (((1,), (1,)), ((), ())), preferred_element_type=jnp.float32
        )
        scores = every[:, :positions]
        for row in range(1, part):
            scores = jnp.where(
                which == row, every[:, row * positions : (row + 1) * positions], scores
            )
        pieces.append(scores)
    scores = jnp.concatenate(pieces, axis=0) * score_scale
    mine = jnp.broadcast_to(len_ref[pl.ds(step, 1), :], (rows, rows))
    diagonal = lax.broadcasted_iota(jnp.int32, (rows, rows), 0) == lax.broadcasted_iota(
        jnp.int32, (rows, rows), 1
    )
    lengths = jnp.sum(jnp.where(diagonal, mine, 0), axis=1, keepdims=True)
    lengths = jnp.concatenate([lengths[g * part : (g + 1) * part] for g, h in order], axis=0)
    in_cache = lax.broadcasted_iota(jnp.int32, scores.shape, 1) < lengths
    scores = jnp.where(in_cache, scores, masked_score)
    top = jnp.maximum(jnp.max(scores, axis=1, keepdims=True), own)
    weights = jnp.where(in_cache, jnp.exp(scores - top), 0.0)
    own_weight = jnp.exp(own - top)
    total = jnp.sum(weights, axis=1, keepdims=True) + own_weight
    added = own_weight * stacked(value_new)
    values_arrive()
    pieces = []
    for g in range(parts):
        mine = weights[g * group : (g + 1) * group]
        blocks = jnp.concatenate(
            [jnp.where(which == row, mine, 0.0).astype(jnp.bfloat16) for row in range(part)],
            axis=1,
        )
        values = near_ref[1, pl.ds(base + g * part, part)].reshape(part * positions, width)
        summed = lax.dot_general(
            blocks, values, (((1,), (0,)), ((), ())), preferred_element_type=jnp.float32
        )
        pieces += [
            summed[h * part : (h + 1) * part, h * HEAD_DIM : (h + 1) * HEAD_DIM]
            for h in range(heads)
        ]
    attended = (jnp.concatenate(pieces, axis=0) + added) / total
    attended = jnp.concatenate(
        [
            jnp.concatenate(
                [
                    attended[(g * heads + h) * part : (g * heads + h + 1) * part]
                    for h in range(heads)
                ],
                axis=1,
            )
            for g in range(parts)
        ],
        axis=0,
    )
    o_ref[pl.ds(base, rows), :] = attended.astype(jnp.bfloat16)


def attend(fresh, lengths, kv):
    _, n, positions, width = kv.shape
    steps = fresh.shape[0]
    inside = pl.BlockSpec(memory_space=pltpu.VMEM)
    return pl.pallas_call(
        attend_kernel,
        in_specs=[inside, inside, pl.BlockSpec(memory_space=pl.ANY)],
        out_specs=inside,
        out_shape=jax.ShapeDtypeStruct((n, width), jnp.bfloat16),
        scratch_shapes=[
            pltpu.VMEM(kv.shape, kv.dtype),
            pltpu.SemaphoreType.DMA((steps, 2)),
        ],
        compiler_params=pltpu.CompilerParams(vmem_limit_bytes=VMEM_LIMIT),
        cost_estimate=pl.CostEstimate(
            flops=4 * n * positions * width,
            bytes_accessed=4 * n * positions * width,
            transcendentals=0,
        ),
    )(fresh, lengths, kv)


def pieces_of(size, most):
    if size % LANES:
        return [(0, size)]
    short = size % most
    pieces = [(0, short)] if short else []
    return pieces + [(at, most) for at in range(short, size, most)]


def expert_kernel(count, outs, mine_ref, *refs):
    slots, (w_ref, d_ref), y_refs = refs[:count], refs[count : count + 2], refs[count + 2 :][:outs]
    x_ref, c_ref, h_ref, in_ref, down_ref, in_sem, down_sem = refs[count + 2 + outs :]
    each = slots[0].shape[0]
    _, width, units = w_ref.shape
    in_cuts, down_cuts = pieces_of(units, 256), pieces_of(width, 512)
    in_copies, down_copies = [], []
    for n, (at, size) in enumerate(in_cuts):
        for half in range(2):
            src, dst = w_ref.at[half], in_ref.at[half]
            if size < units:
                src, dst = src.at[:, pl.ds(at, size)], dst.at[:, pl.ds(at, size)]
            in_copies.append(pltpu.make_async_copy(src, dst, in_sem.at[n, half]))
    for n, (at, size) in enumerate(down_cuts):
        down_copies.append(
            pltpu.make_async_copy(
                d_ref.at[:, pl.ds(at, size)], down_ref.at[:, pl.ds(at, size)], down_sem.at[n]
            )
        )
    copies = [in_copies[2 * n : 2 * n + 2] for n in range(len(in_cuts))]
    copies += [[copy] for copy in down_copies]

    def start(n):
        for copy in copies[n] if n < len(copies) else []:
            copy.start()

    for n in range(AHEAD):
        start(n)
    for n, slot in enumerate(slots):
        place = pl.ds(n * each, each)
        x_ref[place, :] = slot[:, :width]
        gates = slot[:, width:].astype(jnp.float32)
        lane = lax.broadcasted_iota(jnp.int32, gates.shape, 1)
        chosen = jnp.where(lane == mine_ref[0], gates, 0.0)
        c_ref[place, :] = jnp.sum(chosen, axis=1, keepdims=True)

    def keep(n, gate, up):
        at, size = in_cuts[n]
        h_ref[:, at : at + size] = (gate / (1.0 + jnp.exp(-gate)) * up).astype(jnp.bfloat16)

    def give(n, y):
        at, size = down_cuts[n]
        y = (y.astype(jnp.bfloat16).astype(jnp.float32) * c_ref[...]).astype(jnp.bfloat16)
        rows = y.shape[0] // outs
        for m, out in enumerate(y_refs):
            out[:, at : at + size] = y[m * rows : (m + 1) * rows]

    held = None
    for n, (at, size) in enumerate(in_cuts):
        start(n + AHEAD)
        in_copies[2 * n].wait()
        in_copies[2 * n + 1].wait()
        place = slice(at, at + size)
        gate = jnp.dot(x_ref[...], in_ref[0, :, place], preferred_element_type=jnp.float32)
        up = jnp.dot(x_ref[...], in_ref[1, :, place], preferred_element_type=jnp.float32)
        if held is not None:
            keep(*held)
        held = (n, gate, up)
    keep(*held)
    held = None
    for n, (at, size) in enumerate(down_cuts):
        start(len(in_cuts) + n + AHEAD)
        down_copies[n].wait()
        place = slice(at, at + size)
        y = jnp.dot(h_ref[...], down_ref[:, place], preferred_element_type=jnp.float32)
        if held is not None:
            give(*held)
        held = (n, y)
    give(*held)


def expert(slots, outs, mine, w_both, w_down):
    each, packed = slots[0].shape
    rows = each * len(slots)
    _, depth, units = w_both.shape
    width = w_down.shape[1]
    inside = pl.BlockSpec(memory_space=pltpu.VMEM)
    return pl.pallas_call(
        functools.partial(expert_kernel, len(slots), outs),
        in_specs=[pl.BlockSpec(memory_space=pltpu.SMEM)]
        + [inside] * len(slots)
        + [pl.BlockSpec(memory_space=pl.ANY)] * 2,
        out_specs=[inside] * outs,
        scratch_shapes=[
            pltpu.VMEM((rows, depth), jnp.bfloat16),
            pltpu.VMEM((rows, 1), jnp.float32),
            pltpu.VMEM((rows, units), jnp.bfloat16),
            pltpu.VMEM((2, depth, units), jnp.bfloat16),
            pltpu.VMEM((units, width), jnp.bfloat16),
            pltpu.SemaphoreType.DMA((len(pieces_of(units, 256)), 2)),
            pltpu.SemaphoreType.DMA((len(pieces_of(width, 512)),)),
        ],
        out_shape=[jax.ShapeDtypeStruct((rows // outs, width), jnp.bfloat16)] * outs,
        compiler_params=pltpu.CompilerParams(vmem_limit_bytes=VMEM_LIMIT),
        cost_estimate=pl.CostEstimate(
            flops=6 * rows * depth * units,
            bytes_accessed=2 * (3 * depth * units + 2 * rows * depth),
            transcendentals=rows * units,
        ),
    )(mine, *slots, w_both, w_down)


def local(
    hidden_in,
    row_counts,
    qkv_new,
    cache_len,
    kv_cache,
    w_out,
    moe_gain,
    w_in,
    w_down,
    route_ids,
    route_weight,
):
    wide = jnp.float32
    narrow = jnp.bfloat16
    tok_rows, feat_local = hidden_in.shape
    owners = lax.axis_size("ep")
    reps = lax.axis_size("rep")
    parts_seq = lax.axis_size("seq")
    width_local = kv_cache.shape[-1]
    positions = kv_cache.shape[3]
    share_rows = tok_rows // parts_seq
    attend_rows = owners * share_rows
    inner = 2 if owners % 2 == 0 else 1
    outer = owners // inner
    me = lax.axis_index("ep")
    outer_me, inner_me = me // inner, me % inner

    def across(v):
        return lax.ppermute(v, "ep", [(i, i ^ 1) for i in range(owners)])

    def along(v, k):
        pairs = [
            (i, (i // inner + k) % outer * inner + i % inner) for i in range(owners)
        ]
        return lax.ppermute(v, "ep", pairs)

    def other(v):
        return lax.ppermute(v, "rep", [(i, (i + 1) % reps) for i in range(reps)])

    def fence(*values):
        return lax.optimization_barrier(values)

    def rows_of_seq(v, axis):
        return lax.dynamic_slice_in_dim(v, lax.axis_index("seq") * share_rows, share_rows, axis)

    sent = qkv_new.reshape(tok_rows, 3, owners, width_local).transpose(2, 1, 0, 3)
    fresh = lax.all_to_all(sent, "ep", split_axis=0, concat_axis=0, tiled=True)
    fresh = rows_of_seq(fresh, 2)
    tile = math.gcd(attend_rows, ROWS)
    if share_rows != tile:
        fresh = fresh.transpose(0, 2, 1, 3).reshape(attend_rows // tile, tile, 3, width_local)
        fresh = fresh.transpose(0, 2, 1, 3)

    w_both = w_in.transpose(0, 2, 1, 3)
    if inner == 2 and reps == 2:
        half = w_out.shape[0] // 2
        rep_first = lax.axis_index("rep") == 0
        w_mine = jnp.where(rep_first, w_out[:half], w_out[half:])
    else:
        w_mine = w_out
    fresh, w_both, w_mine = fence(fresh, w_both, w_mine)
    w_mine = across(w_mine) if inner == 2 else w_mine

    kv = kv_cache.reshape(2, attend_rows, positions, width_local)
    attended = attend(fresh, cache_len.reshape(attend_rows // tile, tile), kv)
    attended, w_mine = lax.optimization_barrier((attended, w_mine))
    attended = attended.reshape(owners, share_rows, width_local)
    attended = lax.all_gather(attended, "seq", axis=1, tiled=True)

    attended = attended.reshape(outer, inner, tok_rows, width_local)
    if inner == 2:
        first = inner_me == 0
        kept = jnp.where(first, attended[:, 0], attended[:, 1])
        given = jnp.where(first, attended[:, 1], attended[:, 0])
        joined = jnp.concatenate([kept, across(given)], axis=2)
        if reps == 2:
            theirs = other(w_mine)
            both = jnp.concatenate(
                [jnp.where(rep_first, w_mine, theirs), jnp.where(rep_first, theirs, w_mine)],
                axis=0,
            )
        else:
            both = w_mine
        w_pair = jnp.concatenate([w_out, both], axis=0)
    else:
        joined, w_pair = attended[:, 0], w_out
    turned = lax.dynamic_slice_in_dim(
        jnp.concatenate([joined, joined], axis=0), outer_me, outer, 0
    )
    partial_out = jnp.dot(
        turned.reshape(outer * tok_rows, -1), w_pair, preferred_element_type=wide
    ).reshape(outer, tok_rows, feat_local)
    arrived = [along(partial_out[k].astype(narrow), k) for k in range(1, outer)]
    attn_out = partial_out[0]
    for part in arrived:
        attn_out = attn_out + part.astype(wide)
    residual = (hidden_in.astype(wide) + attn_out).astype(narrow)
    residual_wide = residual.astype(wide)

    is_live = jnp.arange(tok_rows, dtype=jnp.int32) < row_counts[0]
    experts_local = w_in.shape[0]
    expert_total = owners * reps * experts_local
    hits = route_ids[:, :, None] == jnp.arange(expert_total, dtype=jnp.int32)[None, None, :]
    hits = hits & is_live[:, None, None]
    coeffs = jnp.sum(jnp.where(hits, route_weight.astype(wide)[:, :, None], 0.0), axis=1)
    lanes = -(-expert_total // LANES) * LANES
    coeffs = jnp.pad(coeffs, ((0, 0), (0, lanes - expert_total))).astype(narrow)
    full_rows = lax.all_gather(residual, "seq", axis=1, tiled=True).astype(wide)
    width = full_rows.shape[1]
    inverse_rms = lax.rsqrt(jnp.mean(full_rows * full_rows, axis=1) + epsilon)
    normed = (full_rows * inverse_rms[:, None] * moe_gain).astype(narrow)
    packed = jnp.concatenate([normed, coeffs], axis=1)
    near = [packed] + [along(packed, k) for k in range(1, outer)]
    far = []
    if inner == 2:
        middle = outer // 2
        far = [across(v) for k, v in enumerate(near) if k != middle or outer == 1]
        if outer > 1:
            *far, near[middle] = fence(*far, near[middle])
            far.insert(middle, across(near[middle]))
    first_expert = (me * reps + lax.axis_index("rep")) * experts_local

    def run_experts(slots):
        if reps == 2:
            slots = slots + [other(s) for s in slots]
        total = None
        for j in range(experts_local):
            mine = jnp.reshape(first_expert + j, (1,)).astype(jnp.int32)
            made = expert(slots, reps, mine, w_both[j], w_down[j])
            total = made if total is None else [t + m for t, m in zip(total, made)]
        if parts_seq > 1:
            total = [
                lax.psum_scatter(t.astype(wide), "seq", scatter_dimension=1, tiled=True).astype(
                    narrow
                )
                for t in total
            ]
        return [t.reshape(outer, tok_rows, feat_local) for t in total]

    def back(v):
        return [along(v[k].astype(narrow), -k) for k in range(1, outer)]

    def summed(first, parts):
        for part in parts:
            first = first + part.astype(wide)
        return first

    made = run_experts(near)
    if inner == 2:
        made, far = fence(made, far)
        swapped = [other(v) for v in made[1:]]
        far_made = run_experts(far)
        far_made, swapped = fence(far_made, swapped)
        far_sum = summed(far_made[0].astype(wide), [other(v) for v in far_made[1:]])
        near_sum = summed(made[0].astype(wide), swapped)
        moe_out, moe_far = near_sum[0], far_sum[0]
        inside = [outer // 2] + [k for k in range(1, outer - 1) if k != outer // 2]
        given = {k: across(far_sum[k].astype(narrow)) for k in inside if outer > 2}
        if outer > 1:
            last = jnp.stack([near_sum[-1], far_sum[-1]]).astype(narrow)
            last = along(last, 1 - outer).astype(wide)
            moe_out, moe_far = moe_out + last[0], moe_far + last[1]
        for k, part in given.items():
            part = near_sum[k] + part.astype(wide)
            moe_out = moe_out + along(part.astype(narrow), -k).astype(wide)
        moe_out = moe_out + across(moe_far.astype(narrow)).astype(wide)
    else:
        near_sum = summed(made[0].astype(wide), [other(v) for v in made[1:]])
        moe_out = summed(near_sum[0], back(near_sum))
    return jnp.where(is_live[:, None], residual_wide + moe_out, 0.0).astype(narrow)


def solution(mesh):
    placed = (
        P(("grp", "ep", "rep"), "seq"),
        P(("grp", "ep", "rep")),
        P(("grp", "ep", "rep"), None, None),
        P("grp", ("rep", "seq")),
        P(None, "grp", ("rep", "seq"), None, "ep"),
        P("ep", "seq"),
        P(),
        P(("ep", "rep"), None, None, "seq"),
        P(("ep", "rep"), "seq", None),
        P(("grp", "ep", "rep"), None),
        P(("grp", "ep", "rep"), None),
    )
    return jax.shard_map(
        local, mesh=mesh, in_specs=placed, out_specs=P(("grp", "ep", "rep"), "seq"), check_vma=False
    )
```

```python
import functools
import math

import jax
import jax.numpy as jnp
from jax import lax
from jax.experimental import pallas as pl
from jax.experimental.pallas import tpu as pltpu
from jax.sharding import PartitionSpec as P

HEAD_DIM = 128
LANES = 128
PART = 8
ROWS = 32
VMEM_LIMIT = 50 << 20
AHEAD = 4
epsilon = 1e-06
masked_score = -1e30


def attend_kernel(fresh_ref, len_ref, kv_ref, o_ref, near_ref, arrived):
    steps, _, rows, width = fresh_ref.shape
    positions = kv_ref.shape[2]

    def copies(step):
        place = pl.ds(pl.multiple_of(step * rows, rows), rows)
        return [
            pltpu.make_async_copy(
                kv_ref.at[n, place], near_ref.at[n, place], arrived.at[step, n]
            )
            for n in range(2)
        ]

    def start(step):
        for copy in copies(step):
            copy.start()

    for step in range(min(AHEAD, steps)):
        start(step)

    @pl.loop(0, steps)
    def _(step):
        @pl.when(step + AHEAD < steps)
        def _():
            start(step + AHEAD)

        keys, values = copies(step)
        attend_rows(step, fresh_ref, len_ref, near_ref, o_ref, keys.wait, values.wait)


def attend_rows(step, fresh_ref, len_ref, near_ref, o_ref, keys_arrive, values_arrive):
    rows, width = fresh_ref.shape[2:]
    positions = near_ref.shape[2]
    heads = width // HEAD_DIM
    part = math.gcd(rows, PART)
    parts = rows // part
    group = heads * part
    base = pl.multiple_of(step * rows, rows)
    q, key_new, value_new = (fresh_ref[step, n].astype(jnp.float32) for n in range(3))
    score_scale = 1.0 / math.sqrt(HEAD_DIM)
    head_of = lax.broadcasted_iota(jnp.int32, (part, width), 1) // HEAD_DIM
    which = lax.broadcasted_iota(jnp.int32, (group, positions), 0) % part
    order = [(g, h) for g in range(parts) for h in range(heads)]

    def stacked(v):
        return jnp.concatenate(
            [
                v[g * part : (g + 1) * part, h * HEAD_DIM : (h + 1) * HEAD_DIM]
                for g, h in order
            ],
            axis=0,
        )

    own = jnp.sum(stacked(q * key_new), axis=1, keepdims=True) * score_scale
    keys_arrive()
    pieces = []
    for g in range(parts):
        mine = q[g * part : (g + 1) * part]
        spread = jnp.concatenate(
            [jnp.where(head_of == h, mine, 0.0) for h in range(heads)], axis=0
        ).astype(jnp.bfloat16)
        keys = near_ref[0, pl.ds(base + g * part, part)].reshape(part * positions, width)
        every = lax.dot_general(
            spread, keys, (((1,), (1,)), ((), ())), preferred_element_type=jnp.float32
        )
        scores = every[:, :positions]
        for row in range(1, part):
            scores = jnp.where(
                which == row, every[:, row * positions : (row + 1) * positions], scores
            )
        pieces.append(scores)
    scores = jnp.concatenate(pieces, axis=0) * score_scale
    mine = jnp.broadcast_to(len_ref[pl.ds(step, 1), :], (rows, rows))
    diagonal = lax.broadcasted_iota(jnp.int32, (rows, rows), 0) == lax.broadcasted_iota(
        jnp.int32, (rows, rows), 1
    )
    lengths = jnp.sum(jnp.where(diagonal, mine, 0), axis=1, keepdims=True)
    lengths = jnp.concatenate([lengths[g * part : (g + 1) * part] for g, h in order], axis=0)
    in_cache = lax.broadcasted_iota(jnp.int32, scores.shape, 1) < lengths
    scores = jnp.where(in_cache, scores, masked_score)
    top = jnp.maximum(jnp.max(scores, axis=1, keepdims=True), own)
    weights = jnp.where(in_cache, jnp.exp(scores - top), 0.0)
    own_weight = jnp.exp(own - top)
    total = jnp.sum(weights, axis=1, keepdims=True) + own_weight
    added = own_weight * stacked(value_new)
    values_arrive()
    pieces = []
    for g in range(parts):
        mine = weights[g * group : (g + 1) * group]
        blocks = jnp.concatenate(
            [jnp.where(which == row, mine, 0.0).astype(jnp.bfloat16) for row in range(part)],
            axis=1,
        )
        values = near_ref[1, pl.ds(base + g * part, part)].reshape(part * positions, width)
        summed = lax.dot_general(
            blocks, values, (((1,), (0,)), ((), ())), preferred_element_type=jnp.float32
        )
        pieces += [
            summed[h * part : (h + 1) * part, h * HEAD_DIM : (h + 1) * HEAD_DIM]
            for h in range(heads)
        ]
    attended = (jnp.concatenate(pieces, axis=0) + added) / total
    attended = jnp.concatenate(
        [
            jnp.concatenate(
                [
                    attended[(g * heads + h) * part : (g * heads + h + 1) * part]
                    for h in range(heads)
                ],
                axis=1,
            )
            for g in range(parts)
        ],
        axis=0,
    )
    o_ref[pl.ds(base, rows), :] = attended.astype(jnp.bfloat16)


def attend(fresh, lengths, kv):
    _, n, positions, width = kv.shape
    steps = fresh.shape[0]
    inside = pl.BlockSpec(memory_space=pltpu.VMEM)
    return pl.pallas_call(
        attend_kernel,
        in_specs=[inside, inside, pl.BlockSpec(memory_space=pl.ANY)],
        out_specs=inside,
        out_shape=jax.ShapeDtypeStruct((n, width), jnp.bfloat16),
        scratch_shapes=[
            pltpu.VMEM(kv.shape, kv.dtype),
            pltpu.SemaphoreType.DMA((steps, 2)),
        ],
        compiler_params=pltpu.CompilerParams(vmem_limit_bytes=VMEM_LIMIT),
        cost_estimate=pl.CostEstimate(
            flops=4 * n * positions * width,
            bytes_accessed=4 * n * positions * width,
            transcendentals=0,
        ),
    )(fresh, lengths, kv)


def pieces_of(size, most):
    if size % LANES:
        return [(0, size)]
    short = size % most
    pieces = [(0, short)] if short else []
    return pieces + [(at, most) for at in range(short, size, most)]


def expert_kernel(count, outs, mine_ref, *refs):
    slots, (w_ref, d_ref), y_refs = refs[:count], refs[count : count + 2], refs[count + 2 :][:outs]
    x_ref, c_ref, h_ref, in_ref, down_ref, in_sem, down_sem = refs[count + 2 + outs :]
    each = slots[0].shape[0]
    _, width, units = w_ref.shape
    in_cuts, down_cuts = pieces_of(units, 256), pieces_of(width, 512)
    in_copies, down_copies = [], []
    for n, (at, size) in enumerate(in_cuts):
        for half in range(2):
            src, dst = w_ref.at[half], in_ref.at[half]
            if size < units:
                src, dst = src.at[:, pl.ds(at, size)], dst.at[:, pl.ds(at, size)]
            in_copies.append(pltpu.make_async_copy(src, dst, in_sem.at[n, half]))
    for n, (at, size) in enumerate(down_cuts):
        down_copies.append(
            pltpu.make_async_copy(
                d_ref.at[:, pl.ds(at, size)], down_ref.at[:, pl.ds(at, size)], down_sem.at[n]
            )
        )
    copies = [in_copies[2 * n : 2 * n + 2] for n in range(len(in_cuts))]
    copies += [[copy] for copy in down_copies]

    def start(n):
        for copy in copies[n] if n < len(copies) else []:
            copy.start()

    for n in range(AHEAD):
        start(n)
    for n, slot in enumerate(slots):
        place = pl.ds(n * each, each)
        x_ref[place, :] = slot[:, :width]
        gates = slot[:, width:].astype(jnp.float32)
        lane = lax.broadcasted_iota(jnp.int32, gates.shape, 1)
        chosen = jnp.where(lane == mine_ref[0], gates, 0.0)
        c_ref[place, :] = jnp.sum(chosen, axis=1, keepdims=True)

    def keep(n, gate, up):
        at, size = in_cuts[n]
        h_ref[:, at : at + size] = (gate / (1.0 + jnp.exp(-gate)) * up).astype(jnp.bfloat16)

    def give(n, y):
        at, size = down_cuts[n]
        y = (y.astype(jnp.bfloat16).astype(jnp.float32) * c_ref[...]).astype(jnp.bfloat16)
        rows = y.shape[0] // outs
        for m, out in enumerate(y_refs):
            out[:, at : at + size] = y[m * rows : (m + 1) * rows]

    held = None
    for n, (at, size) in enumerate(in_cuts):
        start(n + AHEAD)
        in_copies[2 * n].wait()
        in_copies[2 * n + 1].wait()
        place = slice(at, at + size)
        gate = jnp.dot(x_ref[...], in_ref[0, :, place], preferred_element_type=jnp.float32)
        up = jnp.dot(x_ref[...], in_ref[1, :, place], preferred_element_type=jnp.float32)
        if held is not None:
            keep(*held)
        held = (n, gate, up)
    keep(*held)
    held = None
    for n, (at, size) in enumerate(down_cuts):
        start(len(in_cuts) + n + AHEAD)
        down_copies[n].wait()
        place = slice(at, at + size)
        y = jnp.dot(h_ref[...], down_ref[:, place], preferred_element_type=jnp.float32)
        if held is not None:
            give(*held)
        held = (n, y)
    give(*held)


def expert(slots, outs, mine, w_both, w_down):
    each, packed = slots[0].shape
    rows = each * len(slots)
    _, depth, units = w_both.shape
    width = w_down.shape[1]
    inside = pl.BlockSpec(memory_space=pltpu.VMEM)
    return pl.pallas_call(
        functools.partial(expert_kernel, len(slots), outs),
        in_specs=[pl.BlockSpec(memory_space=pltpu.SMEM)]
        + [inside] * len(slots)
        + [pl.BlockSpec(memory_space=pl.ANY)] * 2,
        out_specs=[inside] * outs,
        scratch_shapes=[
            pltpu.VMEM((rows, depth), jnp.bfloat16),
            pltpu.VMEM((rows, 1), jnp.float32),
            pltpu.VMEM((rows, units), jnp.bfloat16),
            pltpu.VMEM((2, depth, units), jnp.bfloat16),
            pltpu.VMEM((units, width), jnp.bfloat16),
            pltpu.SemaphoreType.DMA((len(pieces_of(units, 256)), 2)),
            pltpu.SemaphoreType.DMA((len(pieces_of(width, 512)),)),
        ],
        out_shape=[jax.ShapeDtypeStruct((rows // outs, width), jnp.bfloat16)] * outs,
        compiler_params=pltpu.CompilerParams(vmem_limit_bytes=VMEM_LIMIT),
        cost_estimate=pl.CostEstimate(
            flops=6 * rows * depth * units,
            bytes_accessed=2 * (3 * depth * units + 2 * rows * depth),
            transcendentals=rows * units,
        ),
    )(mine, *slots, w_both, w_down)


def local(
    hidden_in,
    row_counts,
    qkv_new,
    cache_len,
    kv_cache,
    w_out,
    moe_gain,
    w_in,
    w_down,
    route_ids,
    route_weight,
):
    wide = jnp.float32
    narrow = jnp.bfloat16
    tok_rows, feat_local = hidden_in.shape
    owners = lax.axis_size("ep")
    reps = lax.axis_size("rep")
    parts_seq = lax.axis_size("seq")
    width_local = kv_cache.shape[-1]
    positions = kv_cache.shape[3]
    share_rows = tok_rows // parts_seq
    attend_rows = owners * share_rows
    inner = 2 if owners % 2 == 0 else 1
    outer = owners // inner
    me = lax.axis_index("ep")
    outer_me, inner_me = me // inner, me % inner

    def across(v):
        return lax.ppermute(v, "ep", [(i, i ^ 1) for i in range(owners)])

    def along(v, k):
        pairs = [
            (i, (i // inner + k) % outer * inner + i % inner) for i in range(owners)
        ]
        return lax.ppermute(v, "ep", pairs)

    def other(v):
        return lax.ppermute(v, "rep", [(i, (i + 1) % reps) for i in range(reps)])

    def fence(*values):
        return lax.optimization_barrier(values)

    def rows_of_seq(v, axis):
        return lax.dynamic_slice_in_dim(v, lax.axis_index("seq") * share_rows, share_rows, axis)

    sent = qkv_new.reshape(tok_rows, 3, owners, width_local).transpose(2, 1, 0, 3)
    fresh = lax.all_to_all(sent, "ep", split_axis=0, concat_axis=0, tiled=True)
    fresh = rows_of_seq(fresh, 2)
    tile = math.gcd(attend_rows, ROWS)
    if share_rows != tile:
        fresh = fresh.transpose(0, 2, 1, 3).reshape(attend_rows // tile, tile, 3, width_local)
        fresh = fresh.transpose(0, 2, 1, 3)

    w_both = w_in.transpose(0, 2, 1, 3)
    if inner == 2 and reps == 2:
        half = w_out.shape[0] // 2
        rep_first = lax.axis_index("rep") == 0
        w_mine = jnp.where(rep_first, w_out[:half], w_out[half:])
    else:
        w_mine = w_out
    fresh, w_both, w_mine = fence(fresh, w_both, w_mine)
    w_mine = across(w_mine) if inner == 2 else w_mine

    kv = kv_cache.reshape(2, attend_rows, positions, width_local)
    attended = attend(fresh, cache_len.reshape(attend_rows // tile, tile), kv)
    attended, w_mine = lax.optimization_barrier((attended, w_mine))
    attended = attended.reshape(owners, share_rows, width_local)
    attended = lax.all_gather(attended, "seq", axis=1, tiled=True)

    attended = attended.reshape(outer, inner, tok_rows, width_local)
    if inner == 2:
        first = inner_me == 0
        kept = jnp.where(first, attended[:, 0], attended[:, 1])
        given = jnp.where(first, attended[:, 1], attended[:, 0])
        joined = jnp.concatenate([kept, across(given)], axis=2)
        if reps == 2:
            theirs = other(w_mine)
            both = jnp.concatenate(
                [jnp.where(rep_first, w_mine, theirs), jnp.where(rep_first, theirs, w_mine)],
                axis=0,
            )
        else:
            both = w_mine
        w_pair = jnp.concatenate([w_out, both], axis=0)
    else:
        joined, w_pair = attended[:, 0], w_out
    turned = lax.dynamic_slice_in_dim(
        jnp.concatenate([joined, joined], axis=0), outer_me, outer, 0
    )
    partial_out = jnp.dot(
        turned.reshape(outer * tok_rows, -1), w_pair, preferred_element_type=wide
    ).reshape(outer, tok_rows, feat_local)
    partial_out, row_counts = fence(partial_out, row_counts)
    arrived = [along(partial_out[k].astype(narrow), k) for k in range(1, outer)]
    attn_out = partial_out[0]
    for part in arrived:
        attn_out = attn_out + part.astype(wide)
    residual = (hidden_in.astype(wide) + attn_out).astype(narrow)
    residual_wide = residual.astype(wide)

    is_live = jnp.arange(tok_rows, dtype=jnp.int32) < row_counts[0]
    experts_local = w_in.shape[0]
    expert_total = owners * reps * experts_local
    hits = route_ids[:, :, None] == jnp.arange(expert_total, dtype=jnp.int32)[None, None, :]
    hits = hits & is_live[:, None, None]
    coeffs = jnp.sum(jnp.where(hits, route_weight.astype(wide)[:, :, None], 0.0), axis=1)
    lanes = -(-expert_total // LANES) * LANES
    coeffs = jnp.pad(coeffs, ((0, 0), (0, lanes - expert_total))).astype(narrow)
    full_rows = lax.all_gather(residual, "seq", axis=1, tiled=True).astype(wide)
    width = full_rows.shape[1]
    inverse_rms = lax.rsqrt(jnp.mean(full_rows * full_rows, axis=1) + epsilon)
    normed = (full_rows * inverse_rms[:, None] * moe_gain).astype(narrow)
    packed = jnp.concatenate([normed, coeffs], axis=1)
    near = [packed] + [along(packed, k) for k in range(1, outer)]
    far = []
    if inner == 2:
        middle = outer // 2
        far = [across(v) for k, v in enumerate(near) if k != middle or outer == 1]
        if outer > 1:
            *far, near[middle] = fence(*far, near[middle])
            far.insert(middle, across(near[middle]))
    first_expert = (me * reps + lax.axis_index("rep")) * experts_local

    def run_experts(slots):
        if reps == 2:
            slots = slots + [other(s) for s in slots]
        total = None
        for j in range(experts_local):
            mine = jnp.reshape(first_expert + j, (1,)).astype(jnp.int32)
            made = expert(slots, reps, mine, w_both[j], w_down[j])
            total = made if total is None else [t + m for t, m in zip(total, made)]
        if parts_seq > 1:
            total = [
                lax.psum_scatter(t.astype(wide), "seq", scatter_dimension=1, tiled=True).astype(
                    narrow
                )
                for t in total
            ]
        return [t.reshape(outer, tok_rows, feat_local) for t in total]

    def back(v):
        return [along(v[k].astype(narrow), -k) for k in range(1, outer)]

    def summed(first, parts):
        for part in parts:
            first = first + part.astype(wide)
        return first

    made = run_experts(near)
    if inner == 2:
        made, far = fence(made, far)
        swapped = [other(v) for v in made[1:]]
        far_made = run_experts(far)
        far_made, swapped = fence(far_made, swapped)
        far_sum = summed(far_made[0].astype(wide), [other(v) for v in far_made[1:]])
        near_sum = summed(made[0].astype(wide), swapped)
        moe_out, moe_far = near_sum[0], far_sum[0]
        inside = [outer // 2] + [k for k in range(1, outer - 1) if k != outer // 2]
        given = {k: across(far_sum[k].astype(narrow)) for k in inside if outer > 2}
        if outer > 1:
            last = jnp.stack([near_sum[-1], far_sum[-1]]).astype(narrow)
            last = along(last, 1 - outer).astype(wide)
            moe_out, moe_far = moe_out + last[0], moe_far + last[1]
        for k, part in given.items():
            part = near_sum[k] + part.astype(wide)
            moe_out = moe_out + along(part.astype(narrow), -k).astype(wide)
        moe_out = moe_out + across(moe_far.astype(narrow)).astype(wide)
    else:
        near_sum = summed(made[0].astype(wide), [other(v) for v in made[1:]])
        moe_out = summed(near_sum[0], back(near_sum))
    return jnp.where(is_live[:, None], residual_wide + moe_out, 0.0).astype(narrow)


def solution(mesh):
    placed = (
        P(("grp", "ep", "rep"), "seq"),
        P(("grp", "ep", "rep")),
        P(("grp", "ep", "rep"), None, None),
        P("grp", ("rep", "seq")),
        P(None, "grp", ("rep", "seq"), None, "ep"),
        P("ep", "seq"),
        P(),
        P(("ep", "rep"), None, None, "seq"),
        P(("ep", "rep"), "seq", None),
        P(("grp", "ep", "rep"), None),
        P(("grp", "ep", "rep"), None),
    )
    return jax.shard_map(
        local, mesh=mesh, in_specs=placed, out_specs=P(("grp", "ep", "rep"), "seq"), check_vma=False
    )
```

```python
import functools
import math

import jax
import jax.numpy as jnp
from jax import lax
from jax.experimental import pallas as pl
from jax.experimental.pallas import tpu as pltpu
from jax.sharding import PartitionSpec as P

HEAD_DIM = 128
LANES = 128
PART = 8
ROWS = 32
VMEM_LIMIT = 50 << 20
AHEAD = 4
epsilon = 1e-06
masked_score = -1e30


def attend_kernel(fresh_ref, len_ref, kv_ref, o_ref, near_ref, arrived):
    steps, _, rows, width = fresh_ref.shape
    positions = kv_ref.shape[2]

    def copies(step):
        place = pl.ds(pl.multiple_of(step * rows, rows), rows)
        return [
            pltpu.make_async_copy(
                kv_ref.at[n, place], near_ref.at[n, place], arrived.at[step, n]
            )
            for n in range(2)
        ]

    def start(step):
        for copy in copies(step):
            copy.start()

    for step in range(min(AHEAD, steps)):
        start(step)

    @pl.loop(0, steps)
    def _(step):
        @pl.when(step + AHEAD < steps)
        def _():
            start(step + AHEAD)

        keys, values = copies(step)
        attend_rows(step, fresh_ref, len_ref, near_ref, o_ref, keys.wait, values.wait)


def attend_rows(step, fresh_ref, len_ref, near_ref, o_ref, keys_arrive, values_arrive):
    rows, width = fresh_ref.shape[2:]
    positions = near_ref.shape[2]
    heads = width // HEAD_DIM
    part = math.gcd(rows, PART)
    parts = rows // part
    group = heads * part
    base = pl.multiple_of(step * rows, rows)
    q, key_new, value_new = (fresh_ref[step, n].astype(jnp.float32) for n in range(3))
    score_scale = 1.0 / math.sqrt(HEAD_DIM)
    head_of = lax.broadcasted_iota(jnp.int32, (part, width), 1) // HEAD_DIM
    which = lax.broadcasted_iota(jnp.int32, (group, positions), 0) % part
    order = [(g, h) for g in range(parts) for h in range(heads)]

    def stacked(v):
        return jnp.concatenate(
            [
                v[g * part : (g + 1) * part, h * HEAD_DIM : (h + 1) * HEAD_DIM]
                for g, h in order
            ],
            axis=0,
        )

    own = jnp.sum(stacked(q * key_new), axis=1, keepdims=True) * score_scale
    keys_arrive()
    pieces = []
    for g in range(parts):
        mine = q[g * part : (g + 1) * part]
        spread = jnp.concatenate(
            [jnp.where(head_of == h, mine, 0.0) for h in range(heads)], axis=0
        ).astype(jnp.bfloat16)
        keys = near_ref[0, pl.ds(base + g * part, part)].reshape(part * positions, width)
        every = lax.dot_general(
            spread, keys, (((1,), (1,)), ((), ())), preferred_element_type=jnp.float32
        )
        scores = every[:, :positions]
        for row in range(1, part):
            scores = jnp.where(
                which == row, every[:, row * positions : (row + 1) * positions], scores
            )
        pieces.append(scores)
    scores = jnp.concatenate(pieces, axis=0) * score_scale
    mine = jnp.broadcast_to(len_ref[pl.ds(step, 1), :], (rows, rows))
    diagonal = lax.broadcasted_iota(jnp.int32, (rows, rows), 0) == lax.broadcasted_iota(
        jnp.int32, (rows, rows), 1
    )
    lengths = jnp.sum(jnp.where(diagonal, mine, 0), axis=1, keepdims=True)
    lengths = jnp.concatenate([lengths[g * part : (g + 1) * part] for g, h in order], axis=0)
    in_cache = lax.broadcasted_iota(jnp.int32, scores.shape, 1) < lengths
    scores = jnp.where(in_cache, scores, masked_score)
    top = jnp.maximum(jnp.max(scores, axis=1, keepdims=True), own)
    weights = jnp.where(in_cache, jnp.exp(scores - top), 0.0)
    own_weight = jnp.exp(own - top)
    total = jnp.sum(weights, axis=1, keepdims=True) + own_weight
    added = own_weight * stacked(value_new)
    values_arrive()
    pieces = []
    for g in range(parts):
        mine = weights[g * group : (g + 1) * group]
        blocks = jnp.concatenate(
            [jnp.where(which == row, mine, 0.0).astype(jnp.bfloat16) for row in range(part)],
            axis=1,
        )
        values = near_ref[1, pl.ds(base + g * part, part)].reshape(part * positions, width)
        summed = lax.dot_general(
            blocks, values, (((1,), (0,)), ((), ())), preferred_element_type=jnp.float32
        )
        pieces += [
            summed[h * part : (h + 1) * part, h * HEAD_DIM : (h + 1) * HEAD_DIM]
            for h in range(heads)
        ]
    attended = (jnp.concatenate(pieces, axis=0) + added) / total
    attended = jnp.concatenate(
        [
            jnp.concatenate(
                [
                    attended[(g * heads + h) * part : (g * heads + h + 1) * part]
                    for h in range(heads)
                ],
                axis=1,
            )
            for g in range(parts)
        ],
        axis=0,
    )
    o_ref[pl.ds(base, rows), :] = attended.astype(jnp.bfloat16)


def attend(fresh, lengths, kv):
    _, n, positions, width = kv.shape
    steps = fresh.shape[0]
    inside = pl.BlockSpec(memory_space=pltpu.VMEM)
    return pl.pallas_call(
        attend_kernel,
        in_specs=[inside, inside, pl.BlockSpec(memory_space=pl.ANY)],
        out_specs=inside,
        out_shape=jax.ShapeDtypeStruct((n, width), jnp.bfloat16),
        scratch_shapes=[
            pltpu.VMEM(kv.shape, kv.dtype),
            pltpu.SemaphoreType.DMA((steps, 2)),
        ],
        compiler_params=pltpu.CompilerParams(vmem_limit_bytes=VMEM_LIMIT),
        cost_estimate=pl.CostEstimate(
            flops=4 * n * positions * width,
            bytes_accessed=4 * n * positions * width,
            transcendentals=0,
        ),
    )(fresh, lengths, kv)


def pieces_of(size, most):
    if size % LANES:
        return [(0, size)]
    short = size % most
    pieces = [(0, short)] if short else []
    return pieces + [(at, most) for at in range(short, size, most)]


def expert_kernel(count, outs, mine_ref, *refs):
    slots, (w_ref, d_ref), y_refs = refs[:count], refs[count : count + 2], refs[count + 2 :][:outs]
    x_ref, c_ref, h_ref, in_ref, down_ref, in_sem, down_sem = refs[count + 2 + outs :]
    each = slots[0].shape[0]
    _, width, units = w_ref.shape
    in_cuts, down_cuts = pieces_of(units, 256), pieces_of(width, 512)
    in_copies, down_copies = [], []
    for n, (at, size) in enumerate(in_cuts):
        for half in range(2):
            src, dst = w_ref.at[half], in_ref.at[half]
            if size < units:
                src, dst = src.at[:, pl.ds(at, size)], dst.at[:, pl.ds(at, size)]
            in_copies.append(pltpu.make_async_copy(src, dst, in_sem.at[n, half]))
    for n, (at, size) in enumerate(down_cuts):
        down_copies.append(
            pltpu.make_async_copy(
                d_ref.at[:, pl.ds(at, size)], down_ref.at[:, pl.ds(at, size)], down_sem.at[n]
            )
        )
    copies = [in_copies[2 * n : 2 * n + 2] for n in range(len(in_cuts))]
    copies += [[copy] for copy in down_copies]

    def start(n):
        for copy in copies[n] if n < len(copies) else []:
            copy.start()

    for n in range(AHEAD):
        start(n)
    for n, slot in enumerate(slots):
        place = pl.ds(n * each, each)
        x_ref[place, :] = slot[:, :width]
        gates = slot[:, width:].astype(jnp.float32)
        lane = lax.broadcasted_iota(jnp.int32, gates.shape, 1)
        chosen = jnp.where(lane == mine_ref[0], gates, 0.0)
        c_ref[place, :] = jnp.sum(chosen, axis=1, keepdims=True)

    def keep(n, gate, up):
        at, size = in_cuts[n]
        h_ref[:, at : at + size] = (gate / (1.0 + jnp.exp(-gate)) * up).astype(jnp.bfloat16)

    def give(n, y):
        at, size = down_cuts[n]
        y = (y.astype(jnp.bfloat16).astype(jnp.float32) * c_ref[...]).astype(jnp.bfloat16)
        rows = y.shape[0] // outs
        for m, out in enumerate(y_refs):
            out[:, at : at + size] = y[m * rows : (m + 1) * rows]

    held = None
    for n, (at, size) in enumerate(in_cuts):
        start(n + AHEAD)
        in_copies[2 * n].wait()
        in_copies[2 * n + 1].wait()
        place = slice(at, at + size)
        gate = jnp.dot(x_ref[...], in_ref[0, :, place], preferred_element_type=jnp.float32)
        up = jnp.dot(x_ref[...], in_ref[1, :, place], preferred_element_type=jnp.float32)
        if held is not None:
            keep(*held)
        held = (n, gate, up)
    keep(*held)
    held = None
    for n, (at, size) in enumerate(down_cuts):
        start(len(in_cuts) + n + AHEAD)
        down_copies[n].wait()
        place = slice(at, at + size)
        y = jnp.dot(h_ref[...], down_ref[:, place], preferred_element_type=jnp.float32)
        if held is not None:
            give(*held)
        held = (n, y)
    give(*held)


def expert(slots, outs, mine, w_both, w_down):
    each, packed = slots[0].shape
    rows = each * len(slots)
    _, depth, units = w_both.shape
    width = w_down.shape[1]
    inside = pl.BlockSpec(memory_space=pltpu.VMEM)
    return pl.pallas_call(
        functools.partial(expert_kernel, len(slots), outs),
        in_specs=[pl.BlockSpec(memory_space=pltpu.SMEM)]
        + [inside] * len(slots)
        + [pl.BlockSpec(memory_space=pl.ANY)] * 2,
        out_specs=[inside] * outs,
        scratch_shapes=[
            pltpu.VMEM((rows, depth), jnp.bfloat16),
            pltpu.VMEM((rows, 1), jnp.float32),
            pltpu.VMEM((rows, units), jnp.bfloat16),
            pltpu.VMEM((2, depth, units), jnp.bfloat16),
            pltpu.VMEM((units, width), jnp.bfloat16),
            pltpu.SemaphoreType.DMA((len(pieces_of(units, 256)), 2)),
            pltpu.SemaphoreType.DMA((len(pieces_of(width, 512)),)),
        ],
        out_shape=[jax.ShapeDtypeStruct((rows // outs, width), jnp.bfloat16)] * outs,
        compiler_params=pltpu.CompilerParams(vmem_limit_bytes=VMEM_LIMIT),
        cost_estimate=pl.CostEstimate(
            flops=6 * rows * depth * units,
            bytes_accessed=2 * (3 * depth * units + 2 * rows * depth),
            transcendentals=rows * units,
        ),
    )(mine, *slots, w_both, w_down)


def local(
    hidden_in,
    row_counts,
    qkv_new,
    cache_len,
    kv_cache,
    w_out,
    moe_gain,
    w_in,
    w_down,
    route_ids,
    route_weight,
):
    wide = jnp.float32
    narrow = jnp.bfloat16
    tok_rows, feat_local = hidden_in.shape
    owners = lax.axis_size("ep")
    reps = lax.axis_size("rep")
    parts_seq = lax.axis_size("seq")
    width_local = kv_cache.shape[-1]
    positions = kv_cache.shape[3]
    share_rows = tok_rows // parts_seq
    attend_rows = owners * share_rows
    inner = 2 if owners % 2 == 0 else 1
    outer = owners // inner
    me = lax.axis_index("ep")
    outer_me, inner_me = me // inner, me % inner

    def across(v):
        return lax.ppermute(v, "ep", [(i, i ^ 1) for i in range(owners)])

    def along(v, k):
        pairs = [
            (i, (i // inner + k) % outer * inner + i % inner) for i in range(owners)
        ]
        return lax.ppermute(v, "ep", pairs)

    def other(v):
        return lax.ppermute(v, "rep", [(i, (i + 1) % reps) for i in range(reps)])

    def fence(*values):
        return lax.optimization_barrier(values)

    def rows_of_seq(v, axis):
        return lax.dynamic_slice_in_dim(v, lax.axis_index("seq") * share_rows, share_rows, axis)

    sent = qkv_new.reshape(tok_rows, 3, owners, width_local).transpose(2, 1, 0, 3)
    fresh = lax.all_to_all(sent, "ep", split_axis=0, concat_axis=0, tiled=True)
    fresh = rows_of_seq(fresh, 2)
    tile = math.gcd(attend_rows, ROWS)
    if share_rows != tile:
        fresh = fresh.transpose(0, 2, 1, 3).reshape(attend_rows // tile, tile, 3, width_local)
        fresh = fresh.transpose(0, 2, 1, 3)

    w_both = w_in.transpose(0, 2, 1, 3)
    if inner == 2 and reps == 2:
        half = w_out.shape[0] // 2
        rep_first = lax.axis_index("rep") == 0
        w_mine = jnp.where(rep_first, w_out[:half], w_out[half:])
    else:
        w_mine = w_out
    fresh, w_both, w_mine = fence(fresh, w_both, w_mine)
    w_mine = across(w_mine) if inner == 2 else w_mine

    kv = kv_cache.reshape(2, attend_rows, positions, width_local)
    attended = attend(fresh, cache_len.reshape(attend_rows // tile, tile), kv)
    attended, w_mine = lax.optimization_barrier((attended, w_mine))
    attended = attended.reshape(owners, share_rows, width_local)
    attended = lax.all_gather(attended, "seq", axis=1, tiled=True)

    attended = attended.reshape(outer, inner, tok_rows, width_local)
    if inner == 2:
        first = inner_me == 0
        kept = jnp.where(first, attended[:, 0], attended[:, 1])
        given = jnp.where(first, attended[:, 1], attended[:, 0])
        joined = jnp.concatenate([kept, across(given)], axis=2)
        if reps == 2:
            theirs = other(w_mine)
            both = jnp.concatenate(
                [jnp.where(rep_first, w_mine, theirs), jnp.where(rep_first, theirs, w_mine)],
                axis=0,
            )
        else:
            both = w_mine
        w_pair = jnp.concatenate([w_out, both], axis=0)
    else:
        joined, w_pair = attended[:, 0], w_out
    turned = lax.dynamic_slice_in_dim(
        jnp.concatenate([joined, joined], axis=0), outer_me, outer, 0
    )
    partial_out = jnp.dot(
        turned.reshape(outer * tok_rows, -1), w_pair, preferred_element_type=wide
    ).reshape(outer, tok_rows, feat_local)
    partial_out, row_counts = fence(partial_out, row_counts)
    arrived = [along(partial_out[k].astype(narrow), k) for k in range(1, outer)]
    attn_out = partial_out[0]
    for part in arrived:
        attn_out = attn_out + part.astype(wide)
    residual = (hidden_in.astype(wide) + attn_out).astype(narrow)
    residual_wide = residual.astype(wide)

    is_live = jnp.arange(tok_rows, dtype=jnp.int32) < row_counts[0]
    experts_local = w_in.shape[0]
    expert_total = owners * reps * experts_local
    hits = route_ids[:, :, None] == jnp.arange(expert_total, dtype=jnp.int32)[None, None, :]
    hits = hits & is_live[:, None, None]
    coeffs = jnp.sum(jnp.where(hits, route_weight.astype(wide)[:, :, None], 0.0), axis=1)
    lanes = -(-expert_total // LANES) * LANES
    coeffs = jnp.pad(coeffs, ((0, 0), (0, lanes - expert_total))).astype(narrow)
    full_rows = lax.all_gather(residual, "seq", axis=1, tiled=True).astype(wide)
    width = full_rows.shape[1]
    inverse_rms = lax.rsqrt(jnp.mean(full_rows * full_rows, axis=1) + epsilon)
    normed = (full_rows * inverse_rms[:, None] * moe_gain).astype(narrow)
    packed = jnp.concatenate([normed, coeffs], axis=1)
    near = [packed] + [along(packed, k) for k in range(1, outer)]
    far = []
    if inner == 2:
        middle = outer // 2
        far = [across(v) for k, v in enumerate(near) if k != middle or outer == 1]
        if outer > 1:
            *far, near[middle] = fence(*far, near[middle])
            far.insert(middle, across(near[middle]))
    first_expert = (me * reps + lax.axis_index("rep")) * experts_local

    def run_experts(slots, swapped=None):
        if reps == 2:
            slots = slots + (swapped or [other(s) for s in slots])
        total = None
        for j in range(experts_local):
            mine = jnp.reshape(first_expert + j, (1,)).astype(jnp.int32)
            made = expert(slots, reps, mine, w_both[j], w_down[j])
            total = made if total is None else [t + m for t, m in zip(total, made)]
        if parts_seq > 1:
            total = [
                lax.psum_scatter(t.astype(wide), "seq", scatter_dimension=1, tiled=True).astype(
                    narrow
                )
                for t in total
            ]
        return [t.reshape(outer, tok_rows, feat_local) for t in total]

    def back(v):
        return [along(v[k].astype(narrow), -k) for k in range(1, outer)]

    def summed(first, parts):
        for part in parts:
            first = first + part.astype(wide)
        return first

    made = run_experts(near)
    if inner == 2:
        ready = [k for k in range(outer) if k != outer // 2] if reps == 2 else []
        here = {k: other(far[k]) for k in ready}
        made, far, here = fence(made, far, here)
        swapped_far = [here[k] if k in here else other(v) for k, v in enumerate(far)]
        swapped = [other(v) for v in made[1:]]
        far_made = run_experts(far, swapped_far if reps == 2 else None)
        far_made, swapped = fence(far_made, swapped)
        far_sum = summed(far_made[0].astype(wide), [other(v) for v in far_made[1:]])
        near_sum = summed(made[0].astype(wide), swapped)
        moe_out, moe_far = near_sum[0], far_sum[0]
        inside = [outer // 2] + [k for k in range(1, outer - 1) if k != outer // 2]
        given = {k: across(far_sum[k].astype(narrow)) for k in inside if outer > 2}
        if outer > 1:
            last = jnp.stack([near_sum[-1], far_sum[-1]]).astype(narrow)
            last = along(last, 1 - outer).astype(wide)
            moe_out, moe_far = moe_out + last[0], moe_far + last[1]
        for k, part in given.items():
            part = near_sum[k] + part.astype(wide)
            moe_out = moe_out + along(part.astype(narrow), -k).astype(wide)
        moe_out = moe_out + across(moe_far.astype(narrow)).astype(wide)
    else:
        near_sum = summed(made[0].astype(wide), [other(v) for v in made[1:]])
        moe_out = summed(near_sum[0], back(near_sum))
    return jnp.where(is_live[:, None], residual_wide + moe_out, 0.0).astype(narrow)


def solution(mesh):
    placed = (
        P(("grp", "ep", "rep"), "seq"),
        P(("grp", "ep", "rep")),
        P(("grp", "ep", "rep"), None, None),
        P("grp", ("rep", "seq")),
        P(None, "grp", ("rep", "seq"), None, "ep"),
        P("ep", "seq"),
        P(),
        P(("ep", "rep"), None, None, "seq"),
        P(("ep", "rep"), "seq", None),
        P(("grp", "ep", "rep"), None),
        P(("grp", "ep", "rep"), None),
    )
    return jax.shard_map(
        local, mesh=mesh, in_specs=placed, out_specs=P(("grp", "ep", "rep"), "seq"), check_vma=False
    )
```
